32 devices in a mesh: groups: 2 (over y), member: 4 (over x, core), band: 4 (over z).
Axes of the slice: x: 2, y: 2, z: 4, core: 2. Of those that a mesh axis runs over, the one named last changes fastest.
Arguments:
- latent: bfloat16 [8, 256, 1024], P(('groups', 'member'), 'band'), parts along dimension 0, may hold values from -6 to 6
- coef_table: bfloat16 [16, 1024], replicated, may hold values from 0.25 to 2
- out_proj: bfloat16 [25, 1024], replicated, may hold values from -0.1875 to 0.1875
- target: float32 [25, 2048], P(None, ('groups', 'band')), parts along dimension 1, may hold values from -12 to 12
- cell_area: float32 [1024], P('band'), may hold values from 0.2 to 2
- var_weight: float32 [25], replicated, may hold values from 0.5 to 4
- edge_source: int32 [4, 4, 384], replicated, may hold values from 0 to 63
- edge_target: int32 [4, 4, 384], P(None, 'band'), may hold values from 0 to 256, as said below
- edge_weight: int32 [4, 4, 384], replicated, may hold values from 0 to 15
Outputs:
- latent_grad: bfloat16 [8, 256, 1024], P(('groups', 'member'), 'band'), parts along dimension 0
- proj_grad: float32 [50, 1024], P('groups'), parts along dimension 0
- coef_grad: float32 [32, 1024], P('groups'), parts along dimension 0
- mean_loss: float32 [2], P('groups'), parts along dimension 0
The draws below stay inside these ranges and needn't reach their ends.
There are 2 independent parts, one for each index of `groups`. The reference program is written for one: setup_inputs(seed, part) draws one part's arguments, and reference() takes and returns one part's arrays. A program takes and returns all parts, laid end to end along the dimension named above; an argument that names none is the same for every part. Nothing has to cross between parts.
Inputs may be any that keep to these rules, and one draw needn't show every extreme that they name: `edge_target`: A value of 256 marks an unused slot; in each block (s, d) the used slots come first. Every cell of a band is the target of exactly 4 used slots over all source bands. A target band receives at most 384 used slots from one source band, and exactly 384 from some source band.
All inputs are finite; a program needn't handle non-finite values.
Results may differ from the reference program's by a relative error of at most 0.012.
The reference program's roundings to bfloat16 on the way count: a program that leaves them out, or rounds other values in their place, can miss the bound.
Values may be sent and summed in bfloat16 or wider, within the bound.
No kernel may reach another device: no remote copies, remote signals or barrier semaphores. Data moves between devices by JAX's collectives and lax.ppermute only.
A program may use at most 64 MiB of HBM per device.

```python
import math
import jax
import jax.numpy as jnp
from jax import lax

H = 1024
V = 25
NW = 16
K = 4
CELL_DEV = 256
LAT_DEV = 64
CAP = 384
M = 4
LAT = 256
CELLS = 1024
N_BAND = 4


def slot_targets(key):
    base_load = CELL_DEV * K // N_BAND
    key_delta = jax.random.fold_in(key, 101)
    key_order = jax.random.fold_in(key, 102)
    key_cells = jax.random.fold_in(key, 103)
    deltas = jax.random.randint(key_delta, (N_BAND, N_BAND // 2), 0, CAP - base_load + 1)
    deltas = deltas.at[:, 0].set(CAP - base_load)
    paired = jnp.stack([base_load + deltas, base_load - deltas], axis=-1).reshape(N_BAND, N_BAND)
    source_order = jax.vmap(lambda sub_key: jax.random.permutation(sub_key, N_BAND))(jax.random.split(key_order, N_BAND))
    counts = jnp.take_along_axis(paired, source_order, axis=1)
    starts = jnp.cumsum(counts, axis=1) - counts
    slot_index = jnp.arange(CAP)
    where_slot = starts[:, :, None] + slot_index[None, None, :]
    used_slot = slot_index[None, None, :] < counts[:, :, None]
    shuffle = jax.vmap(lambda sub_key: jax.random.permutation(sub_key, CELL_DEV * K))(jax.random.split(key_cells, N_BAND))
    flat_slot = jnp.clip(where_slot, 0, CELL_DEV * K - 1).reshape(N_BAND, N_BAND * CAP)
    picked = jnp.take_along_axis(shuffle, flat_slot, axis=1).reshape(N_BAND, N_BAND, CAP)
    target_cells = jnp.where(used_slot, picked // K, CELL_DEV)
    return jnp.transpose(target_cells, (1, 0, 2)).astype(jnp.int32)


def draw_edge_target(key, part):
    targets = slot_targets(key)
    return targets


def touch_ends(entries, key, smallest, top_value):
    longest = entries.shape.index(max(entries.shape))
    spots = []
    for shift in (0, 1):
        where = [jax.random.randint(jax.random.fold_in(key, axis), (), 0, length) for axis, length in enumerate(entries.shape)]
        where[longest] = (where[longest] + shift) % entries.shape[longest]
        spots.append(tuple(where))
    return entries.at[spots[0]].set(smallest).at[spots[1]].set(top_value)


def steps_of(rng, shape, shards, smallest, top_value):
    gain = 1.0
    for axis_at, shards_of in shards:
        heights = jax.random.uniform(jax.random.fold_in(jax.random.fold_in(rng, 6), axis_at), (shards_of,), jnp.float32, smallest / len(shards), top_value / len(shards))
        gain = gain * jnp.repeat(jnp.exp(heights), shape[axis_at] // shards_of).reshape((-1,) + (1,) * (len(shape) - 1 - axis_at))
    return gain


def centred(key, shape, spread, most, cuts=(), kind=jnp.bfloat16):
    loudness = steps_of(key, shape, cuts, -0.22, 0.18) if cuts else 1.0
    entries = jax.random.normal(key, shape, jnp.float32) * spread * loudness
    return jnp.minimum(jnp.maximum(entries, -most), most).astype(kind)


def setup_inputs(seed: int = 0, part: int = 0) -> dict:
    key_list = jax.random.split(jax.random.key(seed), 10)
    part_splits = jax.random.split(jax.random.fold_in(key_list[9], part), 10)
    return {
        "latent": centred(part_splits[0], (M, LAT, H), 1.0, 6.0, ((0, 4), (1, 4))),
        "coef_table": jnp.clip(jnp.exp(jax.random.uniform(key_list[1], (NW, H), jnp.float32, math.log(0.25), math.log(2.0))), 0.25, 2.0).astype(jnp.bfloat16),
        "out_proj": centred(key_list[2], (V, H), H ** -0.5, 0.1875),
        "target": centred(part_splits[3], (V, CELLS), 2.0, 12.0, ((1, 4),), jnp.float32),
        "cell_area": jnp.clip(jnp.exp(math.log(2.0) - 2.3025851 * jax.random.uniform(key_list[4], (CELLS,), jnp.float32) ** steps_of(key_list[4], (CELLS,), ((0, 4),), -0.2, 0.2)), 0.2, 2.0),
        "var_weight": jnp.clip(jnp.exp(jax.random.uniform(key_list[5], (V,), jnp.float32, math.log(0.5), math.log(4.0))), 0.5, 4.0),
        "edge_source": touch_ends(jax.random.randint(key_list[6], (N_BAND, N_BAND, CAP), 0, LAT_DEV), jax.random.fold_in(key_list[6], 1), 0, LAT_DEV - 1).astype(jnp.int32),
        "edge_target": draw_edge_target(jax.random.fold_in(key_list[9], 71), part),
        "edge_weight": touch_ends(jax.random.randint(key_list[8], (N_BAND, N_BAND, CAP), 0, NW), jax.random.fold_in(key_list[8], 1), 0, NW - 1).astype(jnp.int32),
    }


FAIR_ALPHA = 0.95
SOFTNESS = 0.1
EXACT = lax.Precision.HIGHEST

def soft_abs(values):
    return jnp.sqrt(values * values + SOFTNESS * SOFTNESS) - SOFTNESS

def soft_slope(values):
    return values / jnp.sqrt(values * values + SOFTNESS * SOFTNESS)

def reference(latent, coef_table, out_proj, target, cell_area, var_weight, edge_source, edge_target, edge_weight):
    members = latent.shape[0]
    row_total = latent.shape[1]
    hidden = latent.shape[2]
    bands = edge_source.shape[0]
    variables = target.shape[0]
    cells_all = target.shape[1]
    cells_dev = cells_all // bands
    rows_band = row_total // bands
    table_rows = coef_table.shape[0]
    source_band = jnp.arange(bands, dtype=jnp.int32)[:, None, None]
    target_band = jnp.arange(bands, dtype=jnp.int32)[None, :, None]
    source_rows = (source_band * rows_band + edge_source).reshape(-1).astype(jnp.int32)
    target_rows = jnp.where(edge_target == cells_dev, cells_all, target_band * cells_dev + edge_target).reshape(-1).astype(jnp.int32)
    weight_ids = edge_weight.reshape(-1).astype(jnp.int32)
    edge_scale = coef_table[weight_ids].astype(jnp.float32)
    proj_wide = out_proj.astype(jnp.float32)

    def messages_of(latent_one):
        picked = latent_one[source_rows]
        return (picked, (picked.astype(jnp.float32) * edge_scale).astype(jnp.bfloat16))

    def aggregate_of(messages):
        summed = jax.ops.segment_sum(messages.astype(jnp.float32), target_rows, num_segments=cells_all + 1)
        return summed[:cells_all]

    def forward(latent_one):
        picked, messages = messages_of(latent_one)
        aggregate = aggregate_of(messages)
        return jnp.dot(proj_wide, aggregate.T, precision=EXACT)
    predicted = lax.map(forward, latent)
    weights = var_weight[:, None] * cell_area[None, :]
    pair_coef = FAIR_ALPHA / (members - 1) + (1.0 - FAIR_ALPHA) / members
    error = predicted - target[None]

    def pair_terms(values):
        gaps = values[None] - predicted
        return (lax.optimization_barrier(jnp.sum(soft_abs(gaps), axis=0)), lax.optimization_barrier(jnp.sum(soft_slope(gaps), axis=0)))
    spreads, slope_totals = lax.map(pair_terms, predicted)
    total = jnp.sum(weights * (lax.optimization_barrier(jnp.sum(soft_abs(error), axis=0)) - pair_coef * 0.5 * lax.optimization_barrier(jnp.sum(spreads, axis=0))))
    grad_pred = weights[None] * (soft_slope(error) - pair_coef * slope_totals)

    def backward(inputs):
        latent_one, grad_one = inputs
        picked, messages = messages_of(latent_one)
        aggregate = aggregate_of(messages)
        cell_grad = jnp.dot(grad_one.T, proj_wide, precision=EXACT).astype(jnp.bfloat16)
        cell_grad = jnp.concatenate([cell_grad, jnp.zeros((1, hidden), jnp.bfloat16)], axis=0)
        slot_grad = cell_grad[target_rows].astype(jnp.float32)
        latent_part = jax.ops.segment_sum(slot_grad * edge_scale, source_rows, num_segments=row_total).astype(jnp.bfloat16)
        proj_part = jnp.dot(grad_one, aggregate, precision=EXACT)
        coef_part = jax.ops.segment_sum(slot_grad * picked.astype(jnp.float32), weight_ids, num_segments=table_rows)
        return (latent_part, proj_part, coef_part)
    latent_grad, proj_parts, coef_parts = lax.map(backward, (latent, grad_pred))
    proj_grad = lax.optimization_barrier(jnp.sum(proj_parts, axis=0)) / math.sqrt(members * cells_all)
    coef_grad = lax.optimization_barrier(jnp.sum(coef_parts, axis=0)) / math.sqrt(members * cells_all * K)
    mean_loss = (total / (members * variables * cells_all)).reshape(1)
    return (latent_grad, proj_grad, coef_grad, mean_loss)
```

```python
import functools
import math

import jax
import jax.numpy as jnp
from jax import lax
from jax.experimental import pallas as pl
from jax.experimental.pallas import tpu as pltpu
from jax.sharding import PartitionSpec as P

K = 4
FAIR_ALPHA = 0.95
SOFTNESS = 0.1
F32 = jnp.float32
BF16 = jnp.bfloat16
VMEM = pl.BlockSpec(memory_space=pltpu.VMEM)
PARAMS = pltpu.CompilerParams(vmem_limit_bytes=48 * 1024 * 1024)


def swap(shard, axis, mask):
    peers = lax.axis_size(axis)
    return lax.ppermute(shard, axis, [(i, i ^ mask) for i in range(peers)])


def soft_abs(values):
    return jnp.sqrt(values * values + SOFTNESS * SOFTNESS) - SOFTNESS


def soft_slope(values):
    return values * lax.rsqrt(values * values + SOFTNESS * SOFTNESS)


def up(size, unit):
    return -(-size // unit) * unit


def dot(left, right, left_dim, right_dim):
    return lax.dot_general(
        left, right, (((left_dim,), (right_dim,)), ((), ())), preferred_element_type=F32
    )


def parts(values):
    high = values.astype(BF16)
    rest = values - high.astype(F32)
    mid = rest.astype(BF16)
    low = (rest - mid.astype(F32)).astype(BF16)
    return jnp.concatenate([high, mid, low], axis=0)


def whole(stacked):
    rows = stacked.shape[0] // 3
    return (stacked[:rows] + stacked[rows : 2 * rows]) + stacked[2 * rows :]


def hot(ids, size):
    rows = lax.broadcasted_iota(jnp.int32, (size, ids.shape[1]), 0)
    return jnp.where(rows == ids, 1.0, 0.0).astype(BF16)


def project_kernel(latent, coef, proj, source, weight, target, *out):
    *payloads, products, proj_pad = out
    bands = len(payloads)
    here = lax.axis_index("band")
    rows, hidden = latent.shape
    table = coef.shape[0]
    variables = proj.shape[0]
    proj_pad[...] = jnp.zeros_like(proj_pad)
    proj_pad[0:variables, :] = proj[...]
    wide = latent[...].astype(F32)
    scale = coef[...].astype(F32)
    for q in range(table):
        products[q * rows : (q + 1) * rows, :] = (wide * scale[q : q + 1, :]).astype(BF16)
    projected = dot(proj_pad[...], products[...], 1, 1)
    split = parts(projected)
    for i in range(bands):
        there = lax.bitwise_xor(here, i)
        ids = weight[here, pl.ds(there, 1), :] * rows + source[here, pl.ds(there, 1), :]
        at_slots = whole(dot(split, hot(ids, table * rows), 1, 0))
        cells = target[there, :, :].astype(F32)
        row = lax.broadcasted_iota(jnp.int32, at_slots.shape, 0)
        payloads[i][...] = jnp.where(row == variables, cells, at_slots)


def predict_kernel(variables, *refs):
    *payloads, target, predicted = refs
    bands = len(payloads)
    here = lax.axis_index("band")
    total = 0.0
    for i in range(bands):
        there = lax.bitwise_xor(here, i)
        arrived = payloads[i][...]
        row = lax.broadcasted_iota(jnp.int32, arrived.shape, 0)
        split = parts(jnp.where(row < variables, arrived, 0.0))
        total = total + dot(split, hot(target[there, :, :], predicted.shape[1]), 1, 1)
    predicted[...] = whole(total)


def count_kernel(variables, cells_dev, rows, table, source, weight, *refs):
    *payloads, counts = refs
    here = lax.axis_index("band")
    for i, payload in enumerate(payloads):
        there = lax.bitwise_xor(here, i)
        ids = weight[here, pl.ds(there, 1), :] * rows + source[here, pl.ds(there, 1), :]
        cells = payload[variables : variables + 1, :].astype(jnp.int32)
        block = dot(hot(ids, table * rows), hot(cells, cells_dev), 1, 1)
        counts[:, i * cells_dev : (i + 1) * cells_dev] = block.astype(BF16)


def grade_kernel(pair_coef, target, area, var_weight, *refs):
    *predicted, grad = refs
    members = len(predicted)
    here = lax.axis_index("member")
    variables = target.shape[0]
    wanted = target[...]
    spots = lax.broadcasted_iota(jnp.int32, (variables, variables), 0)
    same = spots == lax.broadcasted_iota(jnp.int32, (variables, variables), 1)
    column = jnp.sum(jnp.where(same, var_weight[...], 0.0), axis=1, keepdims=True)
    weights = column * area[...]
    values = [ref[0:variables, :] for ref in predicted]
    own = values[0]
    slopes = 0.0
    for other in values[1:]:
        slopes = slopes + soft_slope(own - other)
    grad_pred = weights * (soft_slope(own - wanted) - pair_coef * slopes)
    for bit in range(members.bit_length() - 1):
        flip = lax.bitwise_and(lax.shift_right_logical(here, bit), 1) == 1
        ordered = list(values)
        for i in range(members):
            if not i >> bit & 1:
                first, second = values[i], values[i ^ (1 << bit)]
                ordered[i] = jnp.where(flip, second, first)
                ordered[i ^ (1 << bit)] = jnp.where(flip, first, second)
        values = ordered
    loss = 0.0
    spread = 0.0
    for m in range(members):
        loss = loss + soft_abs(values[m] - wanted)
        for k in range(m + 1, members):
            spread = spread + soft_abs(values[m] - values[k])
    total = jnp.sum(weights * (loss - pair_coef * spread), axis=(0, 1), keepdims=True)
    grad[...] = jnp.broadcast_to(total, grad.shape)
    grad[0:variables, :] = grad_pred


def backward_kernel(scale_proj, scale_coef, scale_loss, latent, coef, proj, counts, products, *refs):
    *grads, latent_grad, keep, send, mean_loss, proj_pad, cell_grad, sums = refs
    bands = len(grads)
    band = lax.axis_index("band")
    side = lax.bitwise_and(lax.axis_index("member"), 1)
    variables = proj.shape[0]
    rows, hidden = latent.shape
    table = coef.shape[0]
    cells_dev = grads[0].shape[1]
    padded = grads[0].shape[0]
    proj_pad[...] = jnp.zeros_like(proj_pad)
    proj_pad[0:variables, :] = proj[...]
    lane = lax.broadcasted_iota(jnp.int32, (1, 128), 1)
    losses = jnp.zeros((1, 128), F32)
    pair_grad = jnp.zeros((3 * padded, table * rows), F32)
    for i in range(bands):
        arrived = grads[i][...]
        there = lax.bitwise_xor(band, i)
        losses = losses + jnp.where(lane == there, arrived[variables : variables + 1, 0:128], 0.0)
        row = lax.broadcasted_iota(jnp.int32, arrived.shape, 0)
        split = parts(jnp.where(row < variables, arrived, 0.0))
        pair_grad = pair_grad + dot(split, counts[:, i * cells_dev : (i + 1) * cells_dev], 1, 1)
        three = jnp.concatenate([proj_pad[...]] * 3, axis=0)
        cell_grad[i * cells_dev : (i + 1) * cells_dev, :] = dot(split, three, 0, 0).astype(BF16)
    mean_loss[...] = jnp.sum(losses, axis=1, keepdims=True) * scale_loss
    sums[0:padded, :] = whole(dot(parts(whole(pair_grad)), products[...], 1, 0)) * scale_proj
    step = 256
    for h in range(0, hidden, step):
        block = dot(counts[...], cell_grad[:, h : h + step], 1, 0)
        wide = latent[:, h : h + step].astype(F32)
        scale = coef[:, h : h + step].astype(F32)
        into_latent = 0.0
        for q in range(table):
            piece = block[q * rows : (q + 1) * rows, :]
            into_latent = into_latent + piece * scale[q : q + 1, :]
            sums[padded + q : padded + q + 1, h : h + step] = (
                jnp.sum(piece * wide, axis=0, keepdims=True) * scale_coef
            )
        latent_grad[:, h : h + step] = into_latent.astype(BF16)
    half = hidden // 2
    left, right = sums[:, 0:half], sums[:, half:hidden]
    keep[...] = jnp.where(side == 0, left, right)
    send[...] = jnp.where(side == 0, right, left)


def call(kernel, outs, operands, scratch=(), flops=0):
    return pl.pallas_call(
        kernel,
        out_shape=outs,
        in_specs=[VMEM] * len(operands),
        out_specs=[VMEM] * len(outs),
        scratch_shapes=list(scratch),
        compiler_params=PARAMS,
        cost_estimate=pl.CostEstimate(flops=flops, bytes_accessed=1 << 20, transcendentals=0),
    )(*operands)


def shape(*dims, dtype=F32):
    return jax.ShapeDtypeStruct(dims, dtype)


def local(
    latent,
    coef_table,
    out_proj,
    target,
    cell_area,
    var_weight,
    edge_source,
    edge_target,
    edge_weight,
):
    latent_rows = latent[0]
    rows, hidden = latent_rows.shape
    bands = lax.axis_size("band")
    members = lax.axis_size("member")
    variables, cells_dev = target.shape
    cells_all = cells_dev * bands
    table = coef_table.shape[0]
    slots = edge_source.shape[2]
    pairs = table * rows
    padded = up(variables + 1, 16)
    pair_coef = FAIR_ALPHA / (members - 1) + (1.0 - FAIR_ALPHA) / members

    *payloads, products = call(
        project_kernel,
        [shape(padded, slots)] * bands + [shape(pairs, hidden, dtype=BF16)],
        (latent_rows, coef_table, out_proj, edge_source, edge_weight, edge_target),
        [pltpu.VMEM((padded, hidden), BF16)],
    )
    arrived = [payloads[0]] + [swap(payloads[i], "band", i) for i in range(1, bands)]
    (predicted,) = call(
        functools.partial(predict_kernel, variables),
        [shape(padded, cells_dev)],
        (*arrived, edge_target),
    )
    (counts,) = call(
        functools.partial(count_kernel, variables, cells_dev, rows, table),
        [shape(pairs, cells_all, dtype=BF16)],
        (edge_source, edge_weight, *arrived),
        flops=2 * pairs * slots * cells_all,
    )
    others = [predicted] + [swap(predicted, "member", i) for i in range(1, members)]
    (grad,) = call(
        functools.partial(grade_kernel, pair_coef),
        [shape(padded, cells_dev)],
        (target, cell_area.reshape(1, -1), var_weight.reshape(1, -1), *others),
    )
    grads = [grad] + [swap(grad, "band", i) for i in range(1, bands)]
    latent_grad, keep, send, mean_loss = call(
        functools.partial(
            backward_kernel,
            1.0 / math.sqrt(members * cells_all),
            1.0 / math.sqrt(members * cells_all * K),
            1.0 / (members * variables * cells_all),
        ),
        [
            shape(rows, hidden, dtype=BF16),
            shape(padded + table, hidden // 2),
            shape(padded + table, hidden // 2),
            shape(1, 1),
        ],
        (latent_rows, coef_table, out_proj, counts, products, *grads),
        [
            pltpu.VMEM((padded, hidden), BF16),
            pltpu.VMEM((cells_all, hidden), BF16),
            pltpu.VMEM((padded + table, hidden), F32),
        ],
    )
    total = keep + swap(send, "member", 1)
    step = 2
    while step < members:
        total = total + swap(total, "member", step)
        step *= 2
    step = 1
    while step < bands:
        total = total + swap(total, "band", step)
        step *= 2
    other = swap(total, "member", 1)
    side = lax.bitwise_and(lax.axis_index("member"), 1)
    left = jnp.where(side == 0, total, other)
    right = jnp.where(side == 0, other, total)
    full = jnp.concatenate([left, right], axis=1)
    return (
        latent_grad[None],
        full[:variables],
        full[padded : padded + table],
        mean_loss.reshape(1),
    )


def solution(mesh):
    placed = (
        P(("groups", "member"), "band", None),
        P(),
        P(),
        P(None, ("groups", "band")),
        P("band"),
        P(),
        P(),
        P(None, "band", None),
        P(),
    )
    return jax.shard_map(
        local,
        mesh=mesh,
        in_specs=placed,
        out_specs=(
            P(("groups", "member"), "band", None),
            P("groups", None),
            P("groups", None),
            P("groups"),
        ),
        check_vma=False,
    )
```

```python
import functools
import math

import jax
import jax.numpy as jnp
from jax import lax
from jax.experimental import pallas as pl
from jax.experimental.pallas import tpu as pltpu
from jax.sharding import PartitionSpec as P

K = 4
FAIR_ALPHA = 0.95
SOFTNESS = 0.1
F32 = jnp.float32
BF16 = jnp.bfloat16
VMEM = pl.BlockSpec(memory_space=pltpu.VMEM)
HBM = pl.BlockSpec(memory_space=pltpu.HBM)
PARAMS = pltpu.CompilerParams(vmem_limit_bytes=48 * 1024 * 1024)


def swap(shard, axis, mask):
    peers = lax.axis_size(axis)
    return lax.ppermute(shard, axis, [(i, i ^ mask) for i in range(peers)])


def soft_abs(values):
    return jnp.sqrt(values * values + SOFTNESS * SOFTNESS) - SOFTNESS


def soft_slope(values):
    return values * lax.rsqrt(values * values + SOFTNESS * SOFTNESS)


def up(size, unit):
    return -(-size // unit) * unit


def dot(left, right, left_dim, right_dim):
    return lax.dot_general(
        left, right, (((left_dim,), (right_dim,)), ((), ())), preferred_element_type=F32
    )


def parts(values):
    high = values.astype(BF16)
    rest = values - high.astype(F32)
    mid = rest.astype(BF16)
    low = (rest - mid.astype(F32)).astype(BF16)
    return jnp.concatenate([high, mid, low], axis=0)


def whole(stacked):
    rows = stacked.shape[0] // 3
    return (stacked[:rows] + stacked[rows : 2 * rows]) + stacked[2 * rows :]


def hot(ids, size):
    rows = lax.broadcasted_iota(jnp.int32, (size, ids.shape[1]), 0)
    return jnp.where(rows == ids, 1.0, 0.0).astype(BF16)


def project_kernel(*refs):
    (latent_in, coef_in, proj_in, source_in, weight_in, target_in, wanted_in, area_in, factor_in, *rest) = refs
    *payloads, products, pair_ids, target, wanted, area, factor = rest[:-7]
    latent, coef, proj, source, weight, proj_pad, arrivals = rest[-7:]
    moves = [
        pltpu.make_async_copy(there, here, arrivals.at[n])
        for n, (there, here) in enumerate(
            [
                (latent_in, latent),
                (coef_in, coef),
                (proj_in, proj),
                (source_in, source),
                (weight_in, weight),
                (target_in, target),
                (wanted_in, wanted),
                (area_in, area),
                (factor_in, factor),
            ]
        )
    ]
    for move in moves:
        move.start()
    bands = len(payloads)
    here = lax.axis_index("band")
    rows, hidden = latent.shape
    table = coef.shape[0]
    variables = proj.shape[0]
    proj_pad[...] = jnp.zeros_like(proj_pad)
    for move in moves:
        move.wait()
    proj_pad[0:variables, :] = proj[...]
    wide = latent[...].astype(F32)
    scale = coef[...].astype(F32)
    for q in range(table):
        products[q * rows : (q + 1) * rows, :] = (wide * scale[q : q + 1, :]).astype(BF16)
    projected = dot(proj_pad[...], products[...], 1, 1)
    split = parts(projected)
    for i in range(bands):
        there = lax.bitwise_xor(here, i)
        ids = weight[here, pl.ds(there, 1), :] * rows + source[here, pl.ds(there, 1), :]
        pair_ids[i] = ids
        at_slots = whole(dot(split, hot(ids, table * rows), 1, 0))
        cells = target[there, :, :].astype(F32)
        row = lax.broadcasted_iota(jnp.int32, at_slots.shape, 0)
        payloads[i][...] = jnp.where(row == variables, cells, at_slots)


def predict_kernel(variables, *refs):
    *payloads, target, predicted = refs
    bands = len(payloads)
    here = lax.axis_index("band")
    total = 0.0
    for i in range(bands):
        there = lax.bitwise_xor(here, i)
        arrived = payloads[i][...]
        row = lax.broadcasted_iota(jnp.int32, arrived.shape, 0)
        split = parts(jnp.where(row < variables, arrived, 0.0))
        total = total + dot(split, hot(target[there, :, :], predicted.shape[1]), 1, 1)
    predicted[...] = whole(total)


def count_kernel(variables, cells_dev, pair_ids, *refs):
    *payloads, counts = refs
    for i, payload in enumerate(payloads):
        cells = payload[variables : variables + 1, :].astype(jnp.int32)
        block = dot(hot(pair_ids[i], counts.shape[0]), hot(cells, cells_dev), 1, 1)
        counts[:, i * cells_dev : (i + 1) * cells_dev] = block.astype(BF16)


def grade_kernel(pair_coef, target, area, var_weight, counts, *refs):
    *predicted, grad = refs
    members = len(predicted)
    here = lax.axis_index("member")
    variables = target.shape[0]
    wanted = target[...]
    spots = lax.broadcasted_iota(jnp.int32, (variables, variables), 0)
    same = spots == lax.broadcasted_iota(jnp.int32, (variables, variables), 1)
    column = jnp.sum(jnp.where(same, var_weight[...], 0.0), axis=1, keepdims=True)
    weights = column * area[...]
    values = [ref[0:variables, :] for ref in predicted]
    own = values[0]
    slopes = 0.0
    for other in values[1:]:
        slopes = slopes + soft_slope(own - other)
    grad_pred = weights * (soft_slope(own - wanted) - pair_coef * slopes)
    for bit in range(members.bit_length() - 1):
        flip = lax.bitwise_and(lax.shift_right_logical(here, bit), 1) == 1
        ordered = list(values)
        for i in range(members):
            if not i >> bit & 1:
                first, second = values[i], values[i ^ (1 << bit)]
                ordered[i] = jnp.where(flip, second, first)
                ordered[i ^ (1 << bit)] = jnp.where(flip, first, second)
        values = ordered
    loss = 0.0
    spread = 0.0
    for m in range(members):
        loss = loss + soft_abs(values[m] - wanted)
        for k in range(m + 1, members):
            spread = spread + soft_abs(values[m] - values[k])
    total = jnp.sum(weights * (loss - pair_coef * spread), axis=(0, 1), keepdims=True)
    grad[...] = jnp.broadcast_to(total, grad.shape)
    grad[0:variables, :] = grad_pred


def backward_kernel(scale_proj, scale_coef, scale_loss, latent, coef, proj, counts, products, *refs):
    *grads, latent_grad, keep, send, mean_loss, proj_pad, cell_grad, sums = refs
    bands = len(grads)
    band = lax.axis_index("band")
    side = lax.bitwise_and(lax.axis_index("member"), 1)
    variables = proj.shape[0]
    rows, hidden = latent.shape
    table = coef.shape[0]
    cells_dev = grads[0].shape[1]
    padded = grads[0].shape[0]
    proj_pad[...] = jnp.zeros_like(proj_pad)
    proj_pad[0:variables, :] = proj[...]
    lane = lax.broadcasted_iota(jnp.int32, (1, 128), 1)
    losses = jnp.zeros((1, 128), F32)
    pair_grad = jnp.zeros((3 * padded, table * rows), F32)
    for i in range(bands):
        arrived = grads[i][...]
        there = lax.bitwise_xor(band, i)
        losses = losses + jnp.where(lane == there, arrived[variables : variables + 1, 0:128], 0.0)
        row = lax.broadcasted_iota(jnp.int32, arrived.shape, 0)
        split = parts(jnp.where(row < variables, arrived, 0.0))
        pair_grad = pair_grad + dot(split, counts[:, i * cells_dev : (i + 1) * cells_dev], 1, 1)
        three = jnp.concatenate([proj_pad[...]] * 3, axis=0)
        cell_grad[i * cells_dev : (i + 1) * cells_dev, :] = dot(split, three, 0, 0).astype(BF16)
    mean_loss[...] = jnp.sum(losses, axis=1, keepdims=True) * scale_loss
    sums[0:padded, :] = whole(dot(parts(whole(pair_grad)), products[...], 1, 0)) * scale_proj
    step = 256
    for h in range(0, hidden, step):
        block = dot(counts[...], cell_grad[:, h : h + step], 1, 0)
        wide = latent[:, h : h + step].astype(F32)
        scale = coef[:, h : h + step].astype(F32)
        into_latent = 0.0
        for q in range(table):
            piece = block[q * rows : (q + 1) * rows, :]
            into_latent = into_latent + piece * scale[q : q + 1, :]
            sums[padded + q : padded + q + 1, h : h + step] = (
                jnp.sum(piece * wide, axis=0, keepdims=True) * scale_coef
            )
        latent_grad[:, h : h + step] = into_latent.astype(BF16)
    half = hidden // 2
    left, right = sums[:, 0:half], sums[:, half:hidden]
    keep[...] = jnp.where(side == 0, left, right)
    send[...] = jnp.where(side == 0, right, left)


def write_kernel(scaled, other, latent_grad, mean_loss, *refs):
    latent_out, proj_out, coef_out, loss_out, proj, coef, leaves = refs
    early = [
        pltpu.make_async_copy(latent_grad, latent_out, leaves.at[0]),
        pltpu.make_async_copy(mean_loss, loss_out, leaves.at[1]),
    ]
    for move in early:
        move.start()
    side = lax.bitwise_and(lax.axis_index("member"), 1)
    half = scaled.shape[1]
    variables, table = proj.shape[0], coef.shape[0]
    first = scaled.shape[0] - table
    here, there = scaled[...], other[...]
    left = jnp.where(side == 0, here, there)
    right = jnp.where(side == 0, there, here)
    proj[:, 0:half] = left[0:variables]
    proj[:, half : 2 * half] = right[0:variables]
    coef[:, 0:half] = left[first:]
    coef[:, half : 2 * half] = right[first:]
    late = [
        pltpu.make_async_copy(proj, proj_out, leaves.at[2]),
        pltpu.make_async_copy(coef, coef_out, leaves.at[3]),
    ]
    for move in late:
        move.start()
    for move in early + late:
        move.wait()


def call(kernel, outs, operands, scratch=(), flops=0, source=VMEM, sink=VMEM):
    if source is HBM:
        operands = [pltpu.with_memory_space_constraint(x, pltpu.HBM) for x in operands]
    return pl.pallas_call(
        kernel,
        out_shape=outs,
        in_specs=[source] * len(operands),
        out_specs=[sink] * len(outs),
        scratch_shapes=list(scratch),
        compiler_params=PARAMS,
        cost_estimate=pl.CostEstimate(flops=flops, bytes_accessed=1 << 20, transcendentals=0),
    )(*operands)


def shape(*dims, dtype=F32):
    return jax.ShapeDtypeStruct(dims, dtype)


def local(
    latent,
    coef_table,
    out_proj,
    target,
    cell_area,
    var_weight,
    edge_source,
    edge_target,
    edge_weight,
):
    latent_rows = latent[0]
    rows, hidden = latent_rows.shape
    bands = lax.axis_size("band")
    members = lax.axis_size("member")
    variables, cells_dev = target.shape
    cells_all = cells_dev * bands
    table = coef_table.shape[0]
    slots = edge_source.shape[2]
    pairs = table * rows
    padded = up(variables + 1, 16)
    pair_coef = FAIR_ALPHA / (members - 1) + (1.0 - FAIR_ALPHA) / members

    *payloads, products, pair_ids, cell_ids, wanted, area, factor = call(
        project_kernel,
        [shape(padded, slots)] * bands
        + [
            shape(pairs, hidden, dtype=BF16),
            shape(bands, 1, slots, dtype=jnp.int32),
            shape(bands, 1, slots, dtype=jnp.int32),
            shape(variables, cells_dev),
            shape(1, cells_dev),
            shape(1, variables),
        ],
        (
            latent_rows,
            coef_table,
            out_proj,
            edge_source,
            edge_weight,
            edge_target,
            target,
            cell_area.reshape(1, -1),
            var_weight.reshape(1, -1),
        ),
        [
            pltpu.VMEM((rows, hidden), BF16),
            pltpu.VMEM((table, hidden), BF16),
            pltpu.VMEM((variables, hidden), BF16),
            pltpu.VMEM(edge_source.shape, jnp.int32),
            pltpu.VMEM(edge_weight.shape, jnp.int32),
            pltpu.VMEM((padded, hidden), BF16),
            pltpu.SemaphoreType.DMA((9,)),
        ],
        source=HBM,
    )
    arrived = [payloads[0]] + [swap(payloads[i], "band", i) for i in range(1, bands)]
    (predicted,) = call(
        functools.partial(predict_kernel, variables),
        [shape(padded, cells_dev)],
        (*arrived, cell_ids),
    )
    (counts,) = call(
        functools.partial(count_kernel, variables, cells_dev),
        [shape(pairs, cells_all, dtype=BF16)],
        (pair_ids, *arrived),
        flops=2 * pairs * slots * cells_all,
    )
    members_here = [predicted]
    for i in range(1, members):
        members_here.append(swap(members_here[i ^ 1], "member", 1) if i & 1 else swap(predicted, "member", i))
    (grad,) = call(
        functools.partial(grade_kernel, pair_coef),
        [shape(padded, cells_dev)],
        (wanted, area, factor, counts, *members_here),
    )
    grads = [grad] + [swap(grad, "band", i) for i in range(1, bands)]
    latent_grad, keep, send, mean_loss = call(
        functools.partial(
            backward_kernel,
            1.0 / math.sqrt(members * cells_all),
            1.0 / math.sqrt(members * cells_all * K),
            1.0 / (members * variables * cells_all),
        ),
        [
            shape(rows, hidden, dtype=BF16),
            shape(padded + table, hidden // 2),
            shape(padded + table, hidden // 2),
            shape(1, 1),
        ],
        (latent_rows, coef_table, out_proj, counts, products, *grads),
        [
            pltpu.VMEM((padded, hidden), BF16),
            pltpu.VMEM((cells_all, hidden), BF16),
            pltpu.VMEM((padded + table, hidden), F32),
        ],
    )
    total = keep + swap(send, "member", 1)
    step = 2
    while step < members:
        total = total + swap(total, "member", step)
        step *= 2
    step = 1
    while step < bands:
        total = total + swap(total, "band", step)
        step *= 2
    other = swap(total, "member", 1)
    latent_out, proj_grad, coef_grad, loss_out = call(
        write_kernel,
        [
            shape(rows, hidden, dtype=BF16),
            shape(variables, hidden),
            shape(table, hidden),
            shape(1, 1),
        ],
        (total, other, latent_grad, mean_loss),
        [
            pltpu.VMEM((variables, hidden), F32),
            pltpu.VMEM((table, hidden), F32),
            pltpu.SemaphoreType.DMA((4,)),
        ],
        sink=HBM,
    )
    return (latent_out[None], proj_grad, coef_grad, loss_out.reshape(1))


def solution(mesh):
    placed = (
        P(("groups", "member"), "band", None),
        P(),
        P(),
        P(None, ("groups", "band")),
        P("band"),
        P(),
        P(),
        P(None, "band", None),
        P(),
    )
    return jax.shard_map(
        local,
        mesh=mesh,
        in_specs=placed,
        out_specs=(
            P(("groups", "member"), "band", None),
            P("groups", None),
            P("groups", None),
            P("groups"),
        ),
        check_vma=False,
    )
```

```python
import functools
import math

import jax
import jax.numpy as jnp
from jax import lax
from jax.experimental import pallas as pl
from jax.experimental.pallas import tpu as pltpu
from jax.sharding import PartitionSpec as P

K = 4
FAIR_ALPHA = 0.95
SOFTNESS = 0.1
F32 = jnp.float32
BF16 = jnp.bfloat16
VMEM = pl.BlockSpec(memory_space=pltpu.VMEM)
HBM = pl.BlockSpec(memory_space=pltpu.HBM)
PARAMS = pltpu.CompilerParams(vmem_limit_bytes=48 * 1024 * 1024)


def swap(shard, axis, mask):
    peers = lax.axis_size(axis)
    return lax.ppermute(shard, axis, [(i, i ^ mask) for i in range(peers)])


def soft_abs(values):
    return jnp.sqrt(values * values + SOFTNESS * SOFTNESS) - SOFTNESS


def soft_slope(values):
    return values * lax.rsqrt(values * values + SOFTNESS * SOFTNESS)


def up(size, unit):
    return -(-size // unit) * unit


def dot(left, right, left_dim, right_dim):
    return lax.dot_general(
        left, right, (((left_dim,), (right_dim,)), ((), ())), preferred_element_type=F32
    )


def pieces_of(values):
    high = values.astype(BF16)
    rest = values - high.astype(F32)
    mid = rest.astype(BF16)
    low = (rest - mid.astype(F32)).astype(BF16)
    return high, mid, low


def parts(values):
    return jnp.concatenate(pieces_of(values), axis=0)


def whole(stacked):
    rows = stacked.shape[0] // 3
    return (stacked[:rows] + stacked[rows : 2 * rows]) + stacked[2 * rows :]


def hot(ids, size):
    rows = lax.broadcasted_iota(jnp.int32, (size, ids.shape[1]), 0)
    return jnp.where(rows == ids, 1.0, 0.0).astype(BF16)


def project_kernel(*refs):
    (latent_in, coef_in, proj_in, source_in, weight_in, target_in, wanted_in, area_in, factor_in, *rest) = refs
    *payloads, products, pair_ids, target, wanted, area, factor = rest[:-7]
    latent, coef, proj, source, weight, proj_pad, arrivals = rest[-7:]
    moves = [
        pltpu.make_async_copy(there, here, arrivals.at[n])
        for n, (there, here) in enumerate(
            [
                (latent_in, latent),
                (coef_in, coef),
                (proj_in, proj),
                (source_in, source),
                (weight_in, weight),
                (target_in, target),
                (wanted_in, wanted),
                (area_in, area),
                (factor_in, factor),
            ]
        )
    ]
    for move in moves:
        move.start()
    bands = len(payloads)
    here = lax.axis_index("band")
    rows, hidden = latent.shape
    table = coef.shape[0]
    variables = proj.shape[0]
    proj_pad[...] = jnp.zeros_like(proj_pad)
    for move in moves:
        move.wait()
    proj_pad[0:variables, :] = proj[...]
    wide = latent[...].astype(F32)
    scale = coef[...].astype(F32)
    for q in range(table):
        products[q * rows : (q + 1) * rows, :] = (wide * scale[q : q + 1, :]).astype(BF16)
    projected = dot(proj_pad[...], products[...], 1, 1)
    split = parts(projected)
    for i in range(bands):
        there = lax.bitwise_xor(here, i)
        ids = weight[here, pl.ds(there, 1), :] * rows + source[here, pl.ds(there, 1), :]
        pair_ids[i] = ids
        at_slots = whole(dot(split, hot(ids, table * rows), 1, 0))
        cells = target[there, :, :].astype(F32)
        row = lax.broadcasted_iota(jnp.int32, at_slots.shape, 0)
        payloads[i][...] = jnp.where(row == variables, cells, at_slots)


def predict_kernel(variables, *refs):
    *payloads, target, predicted = refs
    bands = len(payloads)
    here = lax.axis_index("band")
    total = 0.0
    for i in range(bands):
        there = lax.bitwise_xor(here, i)
        arrived = payloads[i][...]
        row = lax.broadcasted_iota(jnp.int32, arrived.shape, 0)
        split = parts(jnp.where(row < variables, arrived, 0.0))
        total = total + dot(split, hot(target[there, :, :], predicted.shape[1]), 1, 1)
    predicted[...] = whole(total)


def count_kernel(variables, cells_dev, pair_ids, *refs):
    *payloads, counts = refs
    for i, payload in enumerate(payloads):
        cells = payload[variables : variables + 1, :].astype(jnp.int32)
        block = dot(hot(pair_ids[i], counts.shape[0]), hot(cells, cells_dev), 1, 1)
        counts[:, i * cells_dev : (i + 1) * cells_dev] = block.astype(BF16)


def grade_kernel(pair_coef, target, area, var_weight, *refs):
    *predicted, grad, rows = refs
    members = len(predicted)
    here = lax.axis_index("member")
    variables = target.shape[0]
    wanted = target[...]
    spots = lax.broadcasted_iota(jnp.int32, (variables, variables), 0)
    same = spots == lax.broadcasted_iota(jnp.int32, (variables, variables), 1)
    column = jnp.sum(jnp.where(same, var_weight[...], 0.0), axis=1, keepdims=True)
    weights = column * area[...]
    values = [ref[0:variables, :] for ref in predicted]
    own = values[0]
    slopes = 0.0
    for other in values[1:]:
        slopes = slopes + soft_slope(own - other)
    grad_pred = weights * (soft_slope(own - wanted) - pair_coef * slopes)
    for bit in range(members.bit_length() - 1):
        flip = lax.bitwise_and(lax.shift_right_logical(here, bit), 1) == 1
        ordered = list(values)
        for i in range(members):
            if not i >> bit & 1:
                first, second = values[i], values[i ^ (1 << bit)]
                ordered[i] = jnp.where(flip, second, first)
                ordered[i ^ (1 << bit)] = jnp.where(flip, first, second)
        values = ordered
    loss = 0.0
    spread = 0.0
    for m in range(members):
        loss = loss + soft_abs(values[m] - wanted)
        for k in range(m + 1, members):
            spread = spread + soft_abs(values[m] - values[k])
    total = jnp.sum(weights * (loss - pair_coef * spread), axis=(0, 1), keepdims=True)
    lane = lax.broadcasted_iota(jnp.int32, rows.shape, 1)
    pieces = [piece.astype(F32) for piece in pieces_of(total)]
    rows[...] = jnp.where(lane == 0, pieces[0], jnp.where(lane == 1, pieces[1], jnp.where(lane == 2, pieces[2], 0.0)))
    rows[0:variables, :] = grad_pred
    grad[...] = rows[...].astype(BF16)


def backward_kernel(scale_proj, scale_coef, scale_loss, latent, coef, proj, counts, products, *refs):
    *grads, latent_grad, keep, send, mean_loss, proj_pad, cell_grad, sums = refs
    bands = len(grads)
    band = lax.axis_index("band")
    side = lax.bitwise_and(lax.axis_index("member"), 1)
    variables = proj.shape[0]
    rows, hidden = latent.shape
    table = coef.shape[0]
    cells_dev = grads[0].shape[1]
    padded = grads[0].shape[0]
    proj_pad[...] = jnp.zeros_like(proj_pad)
    proj_pad[0:variables, :] = proj[...]
    lane = lax.broadcasted_iota(jnp.int32, (1, 128), 1)
    losses = jnp.zeros((1, 128), F32)
    pair_grad = jnp.zeros((padded, table * rows), F32)
    for i in range(bands):
        arrived = grads[i][...].astype(F32)
        there = lax.bitwise_xor(band, i)
        loss = jnp.sum(arrived[variables : variables + 1, 0:128], axis=1, keepdims=True)
        losses = losses + jnp.where(lane == there, loss, 0.0)
        row = lax.broadcasted_iota(jnp.int32, arrived.shape, 0)
        grad = jnp.where(row < variables, arrived, 0.0).astype(BF16)
        pair_grad = pair_grad + dot(grad, counts[:, i * cells_dev : (i + 1) * cells_dev], 1, 1)
        cell_grad[i * cells_dev : (i + 1) * cells_dev, :] = dot(grad, proj_pad[...], 0, 0).astype(BF16)
    mean_loss[...] = jnp.sum(losses, axis=1, keepdims=True) * scale_loss
    sums[0:padded, :] = whole(dot(parts(pair_grad), products[...], 1, 0)) * scale_proj
    step = 256
    for h in range(0, hidden, step):
        block = dot(counts[...], cell_grad[:, h : h + step], 1, 0)
        wide = latent[:, h : h + step].astype(F32)
        scale = coef[:, h : h + step].astype(F32)
        into_latent = 0.0
        for q in range(table):
            piece = block[q * rows : (q + 1) * rows, :]
            into_latent = into_latent + piece * scale[q : q + 1, :]
            sums[padded + q : padded + q + 1, h : h + step] = (
                jnp.sum(piece * wide, axis=0, keepdims=True) * scale_coef
            )
        latent_grad[:, h : h + step] = into_latent.astype(BF16)
    half = hidden // 2
    left, right = sums[:, 0:half], sums[:, half:hidden]
    keep[...] = jnp.where(side == 0, left, right)
    send[...] = jnp.where(side == 0, right, left)


def write_kernel(scaled, other, latent_grad, mean_loss, *refs):
    latent_out, proj_out, coef_out, loss_out, proj, coef, leaves = refs
    early = [
        pltpu.make_async_copy(latent_grad, latent_out, leaves.at[0]),
        pltpu.make_async_copy(mean_loss, loss_out, leaves.at[1]),
    ]
    for move in early:
        move.start()
    side = lax.bitwise_and(lax.axis_index("member"), 1)
    half = scaled.shape[1]
    variables, table = proj.shape[0], coef.shape[0]
    first = scaled.shape[0] - table
    here, there = scaled[...], other[...]
    left = jnp.where(side == 0, here, there)
    right = jnp.where(side == 0, there, here)
    proj[:, 0:half] = left[0:variables]
    proj[:, half : 2 * half] = right[0:variables]
    coef[:, 0:half] = left[first:]
    coef[:, half : 2 * half] = right[first:]
    late = [
        pltpu.make_async_copy(proj, proj_out, leaves.at[2]),
        pltpu.make_async_copy(coef, coef_out, leaves.at[3]),
    ]
    for move in late:
        move.start()
    for move in early + late:
        move.wait()


def call(kernel, outs, operands, scratch=(), flops=0, source=VMEM, sink=VMEM):
    if source is HBM:
        operands = [pltpu.with_memory_space_constraint(x, pltpu.HBM) for x in operands]
    return pl.pallas_call(
        kernel,
        out_shape=outs,
        in_specs=[source] * len(operands),
        out_specs=[sink] * len(outs),
        scratch_shapes=list(scratch),
        compiler_params=PARAMS,
        cost_estimate=pl.CostEstimate(flops=flops, bytes_accessed=1 << 20, transcendentals=0),
    )(*operands)


def shape(*dims, dtype=F32):
    return jax.ShapeDtypeStruct(dims, dtype)


def local(
    latent,
    coef_table,
    out_proj,
    target,
    cell_area,
    var_weight,
    edge_source,
    edge_target,
    edge_weight,
):
    latent_rows = latent[0]
    rows, hidden = latent_rows.shape
    bands = lax.axis_size("band")
    members = lax.axis_size("member")
    variables, cells_dev = target.shape
    cells_all = cells_dev * bands
    table = coef_table.shape[0]
    slots = edge_source.shape[2]
    pairs = table * rows
    padded = up(variables + 1, 16)
    pair_coef = FAIR_ALPHA / (members - 1) + (1.0 - FAIR_ALPHA) / members

    *payloads, products, pair_ids, cell_ids, wanted, area, factor = call(
        project_kernel,
        [shape(padded, slots)] * bands
        + [
            shape(pairs, hidden, dtype=BF16),
            shape(bands, 1, slots, dtype=jnp.int32),
            shape(bands, 1, slots, dtype=jnp.int32),
            shape(variables, cells_dev),
            shape(1, cells_dev),
            shape(1, variables),
        ],
        (
            latent_rows,
            coef_table,
            out_proj,
            edge_source,
            edge_weight,
            edge_target,
            target,
            cell_area.reshape(1, -1),
            var_weight.reshape(1, -1),
        ),
        [
            pltpu.VMEM((rows, hidden), BF16),
            pltpu.VMEM((table, hidden), BF16),
            pltpu.VMEM((variables, hidden), BF16),
            pltpu.VMEM(edge_source.shape, jnp.int32),
            pltpu.VMEM(edge_weight.shape, jnp.int32),
            pltpu.VMEM((padded, hidden), BF16),
            pltpu.SemaphoreType.DMA((9,)),
        ],
        source=HBM,
    )
    arrived = [payloads[0]] + [swap(payloads[i], "band", i) for i in range(1, bands)]
    (predicted,) = call(
        functools.partial(predict_kernel, variables),
        [shape(padded, cells_dev)],
        (*arrived, cell_ids),
    )
    (counts,) = call(
        functools.partial(count_kernel, variables, cells_dev),
        [shape(pairs, cells_all, dtype=BF16)],
        (pair_ids, *arrived),
        flops=2 * pairs * slots * cells_all,
    )
    members_here = [predicted]
    for i in range(1, members):
        members_here.append(swap(members_here[i ^ 1], "member", 1) if i & 1 else swap(predicted, "member", i))
    (grad,) = call(
        functools.partial(grade_kernel, pair_coef),
        [shape(padded, cells_dev, dtype=BF16)],
        (wanted, area, factor, *members_here),
        [pltpu.VMEM((padded, cells_dev), F32)],
    )
    grads = [grad] + [swap(grad, "band", i) for i in range(1, bands)]
    latent_grad, keep, send, mean_loss = call(
        functools.partial(
            backward_kernel,
            1.0 / math.sqrt(members * cells_all),
            1.0 / math.sqrt(members * cells_all * K),
            1.0 / (members * variables * cells_all),
        ),
        [
            shape(rows, hidden, dtype=BF16),
            shape(padded + table, hidden // 2),
            shape(padded + table, hidden // 2),
            shape(1, 1),
        ],
        (latent_rows, coef_table, out_proj, counts, products, *grads),
        [
            pltpu.VMEM((padded, hidden), BF16),
            pltpu.VMEM((cells_all, hidden), BF16),
            pltpu.VMEM((padded + table, hidden), F32),
        ],
    )
    total = keep + swap(send, "member", 1)
    for axis, first, peers in (("member", 2, members), ("band", 1, bands)):
        step = first
        while step < peers:
            rounded = total.astype(BF16)
            total = rounded.astype(F32) + swap(rounded, axis, step).astype(F32)
            step *= 2
    other = swap(total, "member", 1)
    latent_out, proj_grad, coef_grad, loss_out = call(
        write_kernel,
        [
            shape(rows, hidden, dtype=BF16),
            shape(variables, hidden),
            shape(table, hidden),
            shape(1, 1),
        ],
        (total, other, latent_grad, mean_loss),
        [
            pltpu.VMEM((variables, hidden), F32),
            pltpu.VMEM((table, hidden), F32),
            pltpu.SemaphoreType.DMA((4,)),
        ],
        sink=HBM,
    )
    return (latent_out[None], proj_grad, coef_grad, loss_out.reshape(1))


def solution(mesh):
    placed = (
        P(("groups", "member"), "band", None),
        P(),
        P(),
        P(None, ("groups", "band")),
        P("band"),
        P(),
        P(),
        P(None, "band", None),
        P(),
    )
    return jax.shard_map(
        local,
        mesh=mesh,
        in_specs=placed,
        out_specs=(
            P(("groups", "member"), "band", None),
            P("groups", None),
            P("groups", None),
            P("groups"),
        ),
        check_vma=False,
    )
```

```python
import functools
import math

import jax
import jax.numpy as jnp
from jax import lax
from jax.experimental import pallas as pl
from jax.experimental.pallas import tpu as pltpu
from jax.sharding import PartitionSpec as P

K = 4
FAIR_ALPHA = 0.95
SOFTNESS = 0.1
F32 = jnp.float32
BF16 = jnp.bfloat16
VMEM = pl.BlockSpec(memory_space=pltpu.VMEM)
HBM = pl.BlockSpec(memory_space=pltpu.HBM)
PARAMS = pltpu.CompilerParams(vmem_limit_bytes=48 * 1024 * 1024)


def swap(shard, axis, mask):
    peers = lax.axis_size(axis)
    return lax.ppermute(shard, axis, [(i, i ^ mask) for i in range(peers)])


def cross(shard, member_mask, band_mask):
    members, bands = lax.axis_size("member"), lax.axis_size("band")
    pairs = [
        (m * bands + b, (m ^ member_mask) * bands + (b ^ band_mask))
        for m in range(members)
        for b in range(bands)
    ]
    return lax.ppermute(shard, ("member", "band"), pairs)


def odd(value):
    return value.bit_count() & 1


def parity(index, peers):
    found = 0
    for bit in range(peers.bit_length() - 1):
        found = lax.bitwise_xor(found, lax.bitwise_and(lax.shift_right_logical(index, bit), 1))
    return found


def half_here(members, bands):
    return lax.bitwise_xor(parity(lax.axis_index("member"), members), parity(lax.axis_index("band"), bands))


def soft_abs(values):
    return jnp.sqrt(values * values + SOFTNESS * SOFTNESS) - SOFTNESS


def soft_slope(values):
    return values * lax.rsqrt(values * values + SOFTNESS * SOFTNESS)


def up(size, unit):
    return -(-size // unit) * unit


def dot(left, right, left_dim, right_dim):
    return lax.dot_general(
        left, right, (((left_dim,), (right_dim,)), ((), ())), preferred_element_type=F32
    )


def pieces_of(values):
    high = values.astype(BF16)
    rest = values - high.astype(F32)
    mid = rest.astype(BF16)
    low = (rest - mid.astype(F32)).astype(BF16)
    return high, mid, low


def parts(values):
    return jnp.concatenate(pieces_of(values), axis=0)


def whole(stacked):
    rows = stacked.shape[0] // 3
    return (stacked[:rows] + stacked[rows : 2 * rows]) + stacked[2 * rows :]


def hot(ids, size):
    rows = lax.broadcasted_iota(jnp.int32, (size, ids.shape[1]), 0)
    return jnp.where(rows == ids, 1.0, 0.0).astype(BF16)


def project_kernel(*refs):
    (latent_in, coef_in, proj_in, source_in, weight_in, target_in, wanted_in, area_in, factor_in, *rest) = refs
    *payloads, products, pair_ids, target, wanted, area, factor = rest[:-7]
    latent, coef, proj, source, weight, proj_pad, arrivals = rest[-7:]
    moves = [
        pltpu.make_async_copy(there, here, arrivals.at[n])
        for n, (there, here) in enumerate(
            [
                (latent_in, latent),
                (coef_in, coef),
                (proj_in, proj),
                (source_in, source),
                (weight_in, weight),
                (target_in, target),
                (wanted_in, wanted),
                (area_in, area),
                (factor_in, factor),
            ]
        )
    ]
    for move in moves:
        move.start()
    bands = len(payloads)
    here = lax.axis_index("band")
    rows, hidden = latent.shape
    table = coef.shape[0]
    variables = proj.shape[0]
    proj_pad[...] = jnp.zeros_like(proj_pad)
    for move in moves:
        move.wait()
    proj_pad[0:variables, :] = proj[...]
    wide = latent[...].astype(F32)
    scale = coef[...].astype(F32)
    for q in range(table):
        products[q * rows : (q + 1) * rows, :] = (wide * scale[q : q + 1, :]).astype(BF16)
    projected = dot(proj_pad[...], products[...], 1, 1)
    split = parts(projected)
    for i in range(bands):
        there = lax.bitwise_xor(here, i)
        ids = weight[here, pl.ds(there, 1), :] * rows + source[here, pl.ds(there, 1), :]
        pair_ids[i] = ids
        at_slots = whole(dot(split, hot(ids, table * rows), 1, 0))
        cells = target[there, :, :].astype(F32)
        row = lax.broadcasted_iota(jnp.int32, at_slots.shape, 0)
        payloads[i][...] = jnp.where(row == variables, cells, at_slots)


def predict_kernel(variables, *refs):
    *payloads, target, predicted = refs
    payloads = payloads[::-1]
    bands = len(payloads)
    here = lax.axis_index("band")
    total = 0.0
    for i in range(bands):
        there = lax.bitwise_xor(here, i)
        arrived = payloads[i][...]
        row = lax.broadcasted_iota(jnp.int32, arrived.shape, 0)
        split = parts(jnp.where(row < variables, arrived, 0.0))
        total = total + dot(split, hot(target[there, :, :], predicted.shape[1]), 1, 1)
    predicted[...] = whole(total)


def count_kernel(variables, cells_dev, pair_ids, *refs):
    *payloads, counts = refs
    payloads = payloads[::-1]
    for i, payload in enumerate(payloads):
        cells = payload[variables : variables + 1, :].astype(jnp.int32)
        block = dot(hot(pair_ids[i], counts.shape[0]), hot(cells, cells_dev), 1, 1)
        counts[:, i * cells_dev : (i + 1) * cells_dev] = block.astype(BF16)


def grade_kernel(pair_coef, target, area, var_weight, *refs):
    *predicted, grad, rows = refs
    members = len(predicted)
    here = lax.bitwise_xor(lax.axis_index("member"), 1)
    variables = target.shape[0]
    wanted = target[...]
    spots = lax.broadcasted_iota(jnp.int32, (variables, variables), 0)
    same = spots == lax.broadcasted_iota(jnp.int32, (variables, variables), 1)
    column = jnp.sum(jnp.where(same, var_weight[...], 0.0), axis=1, keepdims=True)
    weights = column * area[...]
    values = [ref[0:variables, :] for ref in predicted]
    own = values[0]
    slopes = 0.0
    for other in values[1:]:
        slopes = slopes + soft_slope(own - other)
    grad_pred = weights * (soft_slope(own - wanted) - pair_coef * slopes)
    for bit in range(members.bit_length() - 1):
        flip = lax.bitwise_and(lax.shift_right_logical(here, bit), 1) == 1
        ordered = list(values)
        for i in range(members):
            if not i >> bit & 1:
                first, second = values[i], values[i ^ (1 << bit)]
                ordered[i] = jnp.where(flip, second, first)
                ordered[i ^ (1 << bit)] = jnp.where(flip, first, second)
        values = ordered
    loss = 0.0
    spread = 0.0
    for m in range(members):
        loss = loss + soft_abs(values[m] - wanted)
        for k in range(m + 1, members):
            spread = spread + soft_abs(values[m] - values[k])
    total = jnp.sum(weights * (loss - pair_coef * spread), axis=(0, 1), keepdims=True)
    lane = lax.broadcasted_iota(jnp.int32, rows.shape, 1)
    pieces = [piece.astype(F32) for piece in pieces_of(total)]
    rows[...] = jnp.where(lane == 0, pieces[0], jnp.where(lane == 1, pieces[1], jnp.where(lane == 2, pieces[2], 0.0)))
    rows[0:variables, :] = grad_pred
    grad[...] = rows[...].astype(BF16)


def backward_kernel(members, scale_proj, scale_coef, scale_loss, latent, coef, proj, counts, products, *refs):
    *grads, latent_grad, keep, send, mean_loss, proj_pad, cell_grad, sums = refs
    bands = len(grads)
    band = lax.axis_index("band")
    side = half_here(members, bands)
    variables = proj.shape[0]
    rows, hidden = latent.shape
    table = coef.shape[0]
    cells_dev = grads[0].shape[1]
    padded = grads[0].shape[0]
    proj_pad[...] = jnp.zeros_like(proj_pad)
    proj_pad[0:variables, :] = proj[...]
    lane = lax.broadcasted_iota(jnp.int32, (1, 128), 1)
    losses = jnp.zeros((1, 128), F32)
    pair_grad = jnp.zeros((padded, table * rows), F32)
    for i in range(bands):
        arrived = grads[i][...].astype(F32)
        there = lax.bitwise_xor(band, i)
        loss = jnp.sum(arrived[variables : variables + 1, 0:128], axis=1, keepdims=True)
        losses = losses + jnp.where(lane == there, loss, 0.0)
        row = lax.broadcasted_iota(jnp.int32, arrived.shape, 0)
        grad = jnp.where(row < variables, arrived, 0.0).astype(BF16)
        pair_grad = pair_grad + dot(grad, counts[:, i * cells_dev : (i + 1) * cells_dev], 1, 1)
        cell_grad[i * cells_dev : (i + 1) * cells_dev, :] = dot(grad, proj_pad[...], 0, 0).astype(BF16)
    mean_loss[...] = jnp.sum(losses, axis=1, keepdims=True) * scale_loss
    sums[0:padded, :] = whole(dot(parts(pair_grad), products[...], 1, 0)) * scale_proj
    step = 256
    for h in range(0, hidden, step):
        block = dot(counts[...], cell_grad[:, h : h + step], 1, 0)
        wide = latent[:, h : h + step].astype(F32)
        scale = coef[:, h : h + step].astype(F32)
        into_latent = 0.0
        for q in range(table):
            piece = block[q * rows : (q + 1) * rows, :]
            into_latent = into_latent + piece * scale[q : q + 1, :]
            sums[padded + q : padded + q + 1, h : h + step] = (
                jnp.sum(piece * wide, axis=0, keepdims=True) * scale_coef
            )
        latent_grad[:, h : h + step] = into_latent.astype(BF16)
    half = hidden // 2
    left, right = sums[:, 0:half], sums[:, half:hidden]
    keep[...] = jnp.where(side == 0, left, right)
    send[...] = jnp.where(side == 0, right, left)


def write_kernel(members, bands, variables, scaled, other, latent_grad, mean_loss, *refs):
    latent_out, proj_out, coef_out, loss_out, proj, leaves = refs
    side = half_here(members, bands)
    half = scaled.shape[1]
    first = scaled.shape[0] - coef_out.shape[0]
    here = pl.ds(pl.multiple_of(side * half, half), half)
    there = pl.ds(pl.multiple_of((1 - side) * half, half), half)
    moves = [
        (scaled.at[first:, :], coef_out.at[:, here]),
        (other.at[first:, :], coef_out.at[:, there]),
        (latent_grad, latent_out),
        (mean_loss, loss_out),
        (proj, proj_out),
    ]
    moves = [pltpu.make_async_copy(*move, leaves.at[n]) for n, move in enumerate(moves)]
    for move in moves[:-1]:
        move.start()
    mine, theirs = scaled[0:variables, :], other[0:variables, :]
    proj[:, 0:half] = jnp.where(side == 0, mine, theirs)
    proj[:, half:] = jnp.where(side == 0, theirs, mine)
    moves[-1].start()
    for move in moves:
        move.wait()


def call(kernel, outs, operands, scratch=(), flops=0, source=VMEM, sink=VMEM):
    if source is HBM:
        operands = [pltpu.with_memory_space_constraint(x, pltpu.HBM) for x in operands]
    return pl.pallas_call(
        kernel,
        out_shape=outs,
        in_specs=[source] * len(operands),
        out_specs=[sink] * len(outs),
        scratch_shapes=list(scratch),
        compiler_params=PARAMS,
        cost_estimate=pl.CostEstimate(flops=flops, bytes_accessed=1 << 20, transcendentals=0),
    )(*operands)


def shape(*dims, dtype=F32):
    return jax.ShapeDtypeStruct(dims, dtype)


def local(
    latent,
    coef_table,
    out_proj,
    target,
    cell_area,
    var_weight,
    edge_source,
    edge_target,
    edge_weight,
):
    latent_rows = latent[0]
    rows, hidden = latent_rows.shape
    bands = lax.axis_size("band")
    members = lax.axis_size("member")
    variables, cells_dev = target.shape
    cells_all = cells_dev * bands
    table = coef_table.shape[0]
    slots = edge_source.shape[2]
    pairs = table * rows
    padded = up(variables + 1, 16)
    pair_coef = FAIR_ALPHA / (members - 1) + (1.0 - FAIR_ALPHA) / members

    *payloads, products, pair_ids, cell_ids, wanted, area, factor = call(
        project_kernel,
        [shape(padded, slots)] * bands
        + [
            shape(pairs, hidden, dtype=BF16),
            shape(bands, 1, slots, dtype=jnp.int32),
            shape(bands, 1, slots, dtype=jnp.int32),
            shape(variables, cells_dev),
            shape(1, cells_dev),
            shape(1, variables),
        ],
        (
            latent_rows,
            coef_table,
            out_proj,
            edge_source,
            edge_weight,
            edge_target,
            target,
            cell_area.reshape(1, -1),
            var_weight.reshape(1, -1),
        ),
        [
            pltpu.VMEM((rows, hidden), BF16),
            pltpu.VMEM((table, hidden), BF16),
            pltpu.VMEM((variables, hidden), BF16),
            pltpu.VMEM(edge_source.shape, jnp.int32),
            pltpu.VMEM(edge_weight.shape, jnp.int32),
            pltpu.VMEM((padded, hidden), BF16),
            pltpu.SemaphoreType.DMA((9,)),
        ],
        source=HBM,
    )
    arrived = [cross(payloads[i], 1, i) for i in range(bands)][::-1]
    (predicted,) = call(
        functools.partial(predict_kernel, variables),
        [shape(padded, cells_dev)],
        (*arrived, cell_ids),
    )
    (counts,) = call(
        functools.partial(count_kernel, variables, cells_dev),
        [shape(pairs, cells_all, dtype=BF16)],
        (pair_ids, *arrived),
        flops=2 * pairs * slots * cells_all,
    )
    members_here = [predicted, swap(predicted, "member", 1)]
    for i in range(2, members, 2):
        far = cross(predicted, i + 1, 0)
        members_here += [swap(far, "member", 1), far]
    (grad,) = call(
        functools.partial(grade_kernel, pair_coef),
        [shape(padded, cells_dev, dtype=BF16)],
        (wanted, area, factor, *members_here),
        [pltpu.VMEM((padded, cells_dev), F32)],
    )
    grads = [cross(grad, 1, i) for i in range(bands)]
    latent_grad, keep, send, mean_loss = call(
        functools.partial(
            backward_kernel,
            members,
            1.0 / math.sqrt(members * cells_all),
            1.0 / math.sqrt(members * cells_all * K),
            1.0 / (members * variables * cells_all),
        ),
        [
            shape(rows, hidden, dtype=BF16),
            shape(padded + table, hidden // 2),
            shape(padded + table, hidden // 2),
            shape(1, 1),
        ],
        (latent_rows, coef_table, out_proj, counts, products, *grads),
        [
            pltpu.VMEM((padded, hidden), BF16),
            pltpu.VMEM((cells_all, hidden), BF16),
            pltpu.VMEM((padded + table, hidden), F32),
        ],
    )
    total = keep + swap(send, "member", 1)
    step = 2
    while step < members:
        rounded = total.astype(BF16)
        total = rounded.astype(F32) + cross(rounded, step + 1, 0).astype(F32)
        step *= 2
    step = 1
    while step < bands:
        rounded = total.astype(BF16)
        total = rounded.astype(F32) + cross(rounded, odd(step), step).astype(F32)
        if 2 * step < bands:
            far = [cross(rounded, odd(step * k), step * k).astype(F32) for k in (2, 3)]
            total = total + (far[0] + far[1])
        step *= 4
    other = swap(total, "member", 1)
    latent_out, proj_grad, coef_grad, loss_out = call(
        functools.partial(write_kernel, members, bands, variables),
        [
            shape(rows, hidden, dtype=BF16),
            shape(variables, hidden),
            shape(table, hidden),
            shape(1, 1),
        ],
        (total, other, latent_grad, mean_loss),
        [pltpu.VMEM((variables, hidden), F32), pltpu.SemaphoreType.DMA((5,))],
        sink=HBM,
    )
    return (latent_out[None], proj_grad, coef_grad, loss_out.reshape(1))


def solution(mesh):
    placed = (
        P(("groups", "member"), "band", None),
        P(),
        P(),
        P(None, ("groups", "band")),
        P("band"),
        P(),
        P(),
        P(None, "band", None),
        P(),
    )
    return jax.shard_map(
        local,
        mesh=mesh,
        in_specs=placed,
        out_specs=(
            P(("groups", "member"), "band", None),
            P("groups", None),
            P("groups", None),
            P("groups"),
        ),
        check_vma=False,
    )
```

```python
import functools
import math

import jax
import jax.numpy as jnp
from jax import lax
from jax.experimental import pallas as pl
from jax.experimental.pallas import tpu as pltpu
from jax.sharding import PartitionSpec as P

K = 4
LANES = 128
FAIR_ALPHA = 0.95
SOFTNESS = 0.1
F32 = jnp.float32
BF16 = jnp.bfloat16
VMEM = pl.BlockSpec(memory_space=pltpu.VMEM)
HBM = pl.BlockSpec(memory_space=pltpu.HBM)
PARAMS = pltpu.CompilerParams(vmem_limit_bytes=24 * 1024 * 1024)


def swap(shard, axis, mask):
    peers = lax.axis_size(axis)
    return lax.ppermute(shard, axis, [(i, i ^ mask) for i in range(peers)])


def cross(shard, member_mask, band_mask):
    members, bands = lax.axis_size("member"), lax.axis_size("band")
    pairs = [
        (m * bands + b, (m ^ member_mask) * bands + (b ^ band_mask))
        for m in range(members)
        for b in range(bands)
    ]
    return lax.ppermute(shard, ("member", "band"), pairs)


def odd(value):
    return value.bit_count() & 1


def parity(index, peers):
    found = 0
    for bit in range(peers.bit_length() - 1):
        found = lax.bitwise_xor(found, lax.bitwise_and(lax.shift_right_logical(index, bit), 1))
    return found


def half_here(members, bands):
    return lax.bitwise_xor(parity(lax.axis_index("member"), members), parity(lax.axis_index("band"), bands))


def soft_abs(values):
    return jnp.sqrt(values * values + SOFTNESS * SOFTNESS) - SOFTNESS


def soft_slope(values):
    return values * lax.rsqrt(values * values + SOFTNESS * SOFTNESS)


def up(size, unit):
    return -(-size // unit) * unit


def dot(left, right, left_dim, right_dim):
    return lax.dot_general(
        left, right, (((left_dim,), (right_dim,)), ((), ())), preferred_element_type=F32
    )


def pieces_of(values):
    high = values.astype(BF16)
    rest = values - high.astype(F32)
    mid = rest.astype(BF16)
    low = (rest - mid.astype(F32)).astype(BF16)
    return high, mid, low


def parts(values):
    return jnp.concatenate(pieces_of(values), axis=0)


def whole(stacked):
    rows = stacked.shape[0] // 3
    return (stacked[:rows] + stacked[rows : 2 * rows]) + stacked[2 * rows :]


def hot(ids, size):
    rows = lax.broadcasted_iota(jnp.int32, (size, ids.shape[1]), 0)
    return jnp.where(rows == ids, 1.0, 0.0).astype(BF16)


def pick(table, ids):
    rows, size = table.shape
    slots = ids.shape[1]
    if slots % LANES or size % LANES:
        return [whole(dot(parts(table), hot(ids, size), 1, 0))]
    pieces = []
    for first in range(0, slots, LANES):
        chosen = jnp.broadcast_to(ids[:, first : first + LANES], (rows, LANES))
        lane = lax.rem(chosen, LANES)
        block = lax.div(chosen, LANES)
        found = jnp.zeros((rows, LANES), F32)
        for start in range(0, size, LANES):
            there = jnp.take_along_axis(table[:, start : start + LANES], lane, axis=1, mode="promise_in_bounds")
            found = jnp.where(block == start // LANES, there, found)
        pieces.append(found)
    return pieces


def packed_shape(variables, slots):
    pieces = slots // LANES if slots % LANES == 0 else 1
    return up(pieces * (variables + 1), 8), slots // pieces


def pack(payload, pieces, cells, variables):
    lanes = payload.shape[1]
    full = variables // 8 * 8
    base = len(pieces) * full
    payload[base:, :] = jnp.zeros((payload.shape[0] - base, lanes), F32)
    for n, piece in enumerate(pieces):
        payload[n * full : (n + 1) * full, :] = piece[0:full]
        row = base + n * (variables + 1 - full)
        payload[row : row + variables - full, :] = piece[full:variables]
        payload[row + variables - full : row + variables - full + 1, :] = cells[:, n * lanes : (n + 1) * lanes]


def unpack(payload, variables, slots):
    lanes = payload.shape[1]
    full = variables // 8 * 8
    base = slots // lanes * full
    values, cells = [], []
    for n in range(slots // lanes):
        row = base + n * (variables + 1 - full)
        piece = payload[n * full : (n + 1) * full, :]
        for extra in range(variables - full):
            here = lax.broadcasted_iota(jnp.int32, (8, lanes), 0) == extra
            one = jnp.where(here, payload[row + extra : row + extra + 1, :], 0.0)
            tail = one if extra == 0 else tail + one
        values.append(jnp.concatenate([piece, tail], axis=0) if variables > full else piece)
        cells.append(payload[row + variables - full : row + variables - full + 1, :])
    if len(values) == 1:
        return values[0], cells[0]
    return jnp.concatenate(values, axis=1), jnp.concatenate(cells, axis=1)


def project_kernel(*refs):
    (latent_in, coef_in, proj_in, source_in, weight_in, target_in, wanted_in, area_in, factor_in, *rest) = refs
    *payloads, proj_pad, products, pair_ids, target, wanted, area, factor = rest[:-6]
    latent, coef, proj, source, weight, arrivals = rest[-6:]
    moves = [
        pltpu.make_async_copy(there, here, arrivals.at[n])
        for n, (there, here) in enumerate(
            [
                (latent_in, latent),
                (coef_in, coef),
                (proj_in, proj),
                (source_in, source),
                (weight_in, weight),
                (target_in, target),
                (wanted_in, wanted),
                (area_in, area),
                (factor_in, factor),
            ]
        )
    ]
    for move in moves:
        move.start()
    bands = len(payloads)
    here = lax.axis_index("band")
    rows, hidden = latent.shape
    table = coef.shape[0]
    variables = proj.shape[0]
    proj_pad[...] = jnp.zeros_like(proj_pad)
    for move in moves[:3]:
        move.wait()
    proj_pad[0:variables, :] = proj[...]
    wide = latent[...].astype(F32)
    scale = coef[...].astype(F32)
    for q in range(table):
        products[q * rows : (q + 1) * rows, :] = (wide * scale[q : q + 1, :]).astype(BF16)
    projected = dot(proj_pad[...], products[...], 1, 1)
    for move in moves[3:]:
        move.wait()
    for i in range(bands):
        there = lax.bitwise_xor(here, i)
        ids = weight[here, pl.ds(there, 1), :] * rows + source[here, pl.ds(there, 1), :]
        pair_ids[i] = ids
        pack(payloads[i], pick(projected, ids), target[there, :, :].astype(F32), variables)


def predict_kernel(variables, *refs):
    *payloads, target, predicted = refs
    payloads = payloads[::-1]
    bands = len(payloads)
    here = lax.axis_index("band")
    total = 0.0
    for i in range(bands):
        there = lax.bitwise_xor(here, i)
        arrived, _ = unpack(payloads[i], variables, target.shape[2])
        total = total + dot(parts(arrived), hot(target[there, :, :], predicted.shape[1]), 1, 1)
    predicted[...] = whole(total)


def count_kernel(variables, cells_dev, pair_ids, *refs):
    *payloads, counts = refs
    payloads = payloads[::-1]
    for i, payload in enumerate(payloads):
        cells = unpack(payload, variables, pair_ids.shape[2])[1].astype(jnp.int32)
        block = dot(hot(pair_ids[i], counts.shape[0]), hot(cells, cells_dev), 1, 1)
        counts[:, i * cells_dev : (i + 1) * cells_dev] = block.astype(BF16)


def grade_kernel(pair_coef, target, area, var_weight, *refs):
    *predicted, grad, rows = refs
    members = len(predicted)
    here = lax.bitwise_xor(lax.axis_index("member"), 1)
    variables = target.shape[0]
    wanted = target[...]
    spots = lax.broadcasted_iota(jnp.int32, (variables, variables), 0)
    same = spots == lax.broadcasted_iota(jnp.int32, (variables, variables), 1)
    column = jnp.sum(jnp.where(same, var_weight[...], 0.0), axis=1, keepdims=True)
    weights = column * area[...]
    values = [ref[0:variables, :] for ref in predicted]
    own = values[0]
    slopes = 0.0
    for other in values[1:]:
        slopes = slopes + soft_slope(own - other)
    grad_pred = weights * (soft_slope(own - wanted) - pair_coef * slopes)
    for bit in range(members.bit_length() - 1):
        flip = lax.bitwise_and(lax.shift_right_logical(here, bit), 1) == 1
        ordered = list(values)
        for i in range(members):
            if not i >> bit & 1:
                first, second = values[i], values[i ^ (1 << bit)]
                ordered[i] = jnp.where(flip, second, first)
                ordered[i ^ (1 << bit)] = jnp.where(flip, first, second)
        values = ordered
    loss = 0.0
    spread = 0.0
    for m in range(members):
        loss = loss + soft_abs(values[m] - wanted)
        for k in range(m + 1, members):
            spread = spread + soft_abs(values[m] - values[k])
    total = jnp.sum(weights * (loss - pair_coef * spread), axis=(0, 1), keepdims=True)
    lane = lax.broadcasted_iota(jnp.int32, rows.shape, 1)
    pieces = [piece.astype(F32) for piece in pieces_of(total)]
    rows[...] = jnp.where(lane == 0, pieces[0], jnp.where(lane == 1, pieces[1], jnp.where(lane == 2, pieces[2], 0.0)))
    rows[0:variables, :] = grad_pred
    grad[...] = rows[...].astype(BF16)


def back_to_pairs(grad, proj, counts):
    return dot(grad, proj, 0, 0).astype(BF16), dot(grad, counts, 1, 1)


def only_grads(arrived, variables):
    row = lax.broadcasted_iota(jnp.int32, arrived.shape, 0)
    return jnp.where(row < variables, arrived.astype(F32), 0.0).astype(BF16)


def early_kernel(index, variables, proj, counts, grad, *refs):
    *before, pair_grad, block, cell_grad = refs
    cells_dev = grad.shape[1]
    own = counts[:, index * cells_dev : (index + 1) * cells_dev]
    cell_grad[...], pairs_here = back_to_pairs(only_grads(grad[...], variables), proj[...], own)
    pair_grad[...] = before[0][...] + pairs_here if before else pairs_here
    step = 256
    for h in range(0, block.shape[1], step):
        here = dot(own, cell_grad[:, h : h + step], 1, 0)
        block[:, h : h + step] = before[1][:, h : h + step] + here if before else here


def backward_kernel(members, variables, early, scale_proj, scale_coef, scale_loss, latent, coef, proj, counts, products, *refs):
    near_pair_grad, near_block, *grads = refs[:-6]
    latent_grad, keep, send, mean_loss, cell_grad, sums = refs[-6:]
    bands = len(grads)
    band = lax.axis_index("band")
    side = half_here(members, bands)
    rows, hidden = latent.shape
    table = coef.shape[0]
    cells_dev = grads[0].shape[1]
    padded = grads[0].shape[0]
    lane = lax.broadcasted_iota(jnp.int32, (1, 128), 1)
    losses = jnp.zeros((1, 128), F32)
    pair_grad = near_pair_grad[...]
    for i in range(bands):
        there = lax.bitwise_xor(band, i)
        loss = jnp.sum(grads[i][variables : variables + 1, 0:128].astype(F32), axis=1, keepdims=True)
        losses = losses + jnp.where(lane == there, loss, 0.0)
        if i not in early:
            spot = slice((i - 1) * cells_dev, i * cells_dev)
            cell_grad[spot, :], here = back_to_pairs(
                only_grads(grads[i][...], variables),
                proj[...],
                counts[:, i * cells_dev : (i + 1) * cells_dev],
            )
            pair_grad = pair_grad + here
    mean_loss[...] = jnp.sum(losses, axis=1, keepdims=True) * scale_loss
    sums[0:padded, :] = whole(dot(parts(pair_grad), products[...], 1, 0)) * scale_proj
    step = 256
    for h in range(0, hidden, step):
        block = near_block[:, h : h + step] + dot(counts[:, cells_dev : cells_dev + cell_grad.shape[0]], cell_grad[:, h : h + step], 1, 0)
        wide = latent[:, h : h + step].astype(F32)
        scale = coef[:, h : h + step].astype(F32)
        into_latent = 0.0
        for q in range(table):
            piece = block[q * rows : (q + 1) * rows, :]
            into_latent = into_latent + piece * scale[q : q + 1, :]
            sums[padded + q : padded + q + 1, h : h + step] = (
                jnp.sum(piece * wide, axis=0, keepdims=True) * scale_coef
            )
        latent_grad[:, h : h + step] = into_latent.astype(BF16)
    half = hidden // 2
    left, right = sums[:, 0:half], sums[:, half:hidden]
    keep[...] = jnp.where(side == 0, left, right)
    send[...] = jnp.where(side == 0, right, left)


def write_kernel(members, bands, variables, scaled, other, latent_grad, mean_loss, *refs):
    latent_out, proj_out, coef_out, loss_out, proj, leaves = refs
    side = half_here(members, bands)
    half = scaled.shape[1]
    first = scaled.shape[0] - coef_out.shape[0]
    here = pl.ds(pl.multiple_of(side * half, half), half)
    there = pl.ds(pl.multiple_of((1 - side) * half, half), half)
    moves = [
        (scaled.at[first:, :], coef_out.at[:, here]),
        (other.at[first:, :], coef_out.at[:, there]),
        (latent_grad, latent_out),
        (mean_loss, loss_out),
        (proj, proj_out),
    ]
    moves = [pltpu.make_async_copy(*move, leaves.at[n]) for n, move in enumerate(moves)]
    for move in moves[:-1]:
        move.start()
    mine, theirs = scaled[0:variables, :], other[0:variables, :]
    proj[:, 0:half] = jnp.where(side == 0, mine, theirs)
    proj[:, half:] = jnp.where(side == 0, theirs, mine)
    moves[-1].start()
    for move in moves:
        move.wait()


def call(kernel, outs, operands, scratch=(), flops=0, source=VMEM, sink=VMEM):
    if source is HBM:
        operands = [pltpu.with_memory_space_constraint(x, pltpu.HBM) for x in operands]
    return pl.pallas_call(
        kernel,
        out_shape=outs,
        in_specs=[source] * len(operands),
        out_specs=[sink] * len(outs),
        scratch_shapes=list(scratch),
        compiler_params=PARAMS,
        cost_estimate=pl.CostEstimate(flops=flops, bytes_accessed=1 << 20, transcendentals=0),
    )(*operands)


def shape(*dims, dtype=F32):
    return jax.ShapeDtypeStruct(dims, dtype)


def local(
    latent,
    coef_table,
    out_proj,
    target,
    cell_area,
    var_weight,
    edge_source,
    edge_target,
    edge_weight,
):
    latent_rows = latent[0]
    rows, hidden = latent_rows.shape
    bands = lax.axis_size("band")
    members = lax.axis_size("member")
    variables, cells_dev = target.shape
    cells_all = cells_dev * bands
    table = coef_table.shape[0]
    slots = edge_source.shape[2]
    pairs = table * rows
    padded = up(variables + 1, 16)
    pair_coef = FAIR_ALPHA / (members - 1) + (1.0 - FAIR_ALPHA) / members

    *payloads, proj_pad, products, pair_ids, cell_ids, wanted, area, factor = call(
        project_kernel,
        [shape(*packed_shape(variables, slots))] * bands
        + [
            shape(padded, hidden, dtype=BF16),
            shape(pairs, hidden, dtype=BF16),
            shape(bands, 1, slots, dtype=jnp.int32),
            shape(bands, 1, slots, dtype=jnp.int32),
            shape(variables, cells_dev),
            shape(1, cells_dev),
            shape(1, variables),
        ],
        (
            latent_rows,
            coef_table,
            out_proj,
            edge_source,
            edge_weight,
            edge_target,
            target,
            cell_area.reshape(1, -1),
            var_weight.reshape(1, -1),
        ),
        [
            pltpu.VMEM((rows, hidden), BF16),
            pltpu.VMEM((table, hidden), BF16),
            pltpu.VMEM((variables, hidden), BF16),
            pltpu.VMEM(edge_source.shape, jnp.int32),
            pltpu.VMEM(edge_weight.shape, jnp.int32),
            pltpu.SemaphoreType.DMA((9,)),
        ],
        source=HBM,
    )
    arrived = [cross(payloads[i], 1, i) for i in range(bands)][::-1]
    (predicted,) = call(
        functools.partial(predict_kernel, variables),
        [shape(up(variables, 8), cells_dev)],
        (*arrived, cell_ids),
    )
    (counts,) = call(
        functools.partial(count_kernel, variables, cells_dev),
        [shape(pairs, cells_all, dtype=BF16)],
        (pair_ids, *arrived),
        flops=2 * pairs * slots * cells_all,
    )
    members_here = [predicted, swap(predicted, "member", 1)]
    for i in range(2, members, 2):
        far = cross(predicted, i + 1, 0)
        if i == 2:
            far, counts = lax.optimization_barrier((far, counts))
        members_here += [swap(far, "member", 1), far]
    (grad,) = call(
        functools.partial(grade_kernel, pair_coef),
        [shape(padded, cells_dev, dtype=BF16)],
        (wanted, area, factor, *members_here),
        [pltpu.VMEM((padded, cells_dev), F32)],
    )
    grads = [cross(grad, 1, i) for i in range(bands)]
    early = sorted({0, bands - 1})
    sums = ()
    for index in early:
        sums = call(
            functools.partial(early_kernel, index, variables),
            [shape(padded, pairs), shape(pairs, hidden)],
            (proj_pad, counts, grads[index], *sums),
            [pltpu.VMEM((cells_dev, hidden), BF16)],
            flops=2 * pairs * cells_dev * hidden,
        )
    latent_grad, keep, send, mean_loss = call(
        functools.partial(
            backward_kernel,
            members,
            variables,
            early,
            1.0 / math.sqrt(members * cells_all),
            1.0 / math.sqrt(members * cells_all * K),
            1.0 / (members * variables * cells_all),
        ),
        [
            shape(rows, hidden, dtype=BF16),
            shape(padded + table, hidden // 2),
            shape(padded + table, hidden // 2),
            shape(1, 1),
        ],
        (latent_rows, coef_table, proj_pad, counts, products, *sums, *grads),
        [
            pltpu.VMEM((cells_all - len(early) * cells_dev, hidden), BF16),
            pltpu.VMEM((padded + table, hidden), F32),
        ],
    )
    total = keep + swap(send, "member", 1)
    step = 2
    while step < members:
        rounded = total.astype(BF16)
        total = rounded.astype(F32) + cross(rounded, step + 1, 0).astype(F32)
        step *= 2
    step = 1
    while step < bands:
        rounded = total.astype(BF16)
        total = rounded.astype(F32) + cross(rounded, odd(step), step).astype(F32)
        if 2 * step < bands:
            far = [cross(rounded, odd(step * k), step * k).astype(F32) for k in (2, 3)]
            total = total + (far[0] + far[1])
        step *= 4
    other = swap(total, "member", 1)
    latent_out, proj_grad, coef_grad, loss_out = call(
        functools.partial(write_kernel, members, bands, variables),
        [
            shape(rows, hidden, dtype=BF16),
            shape(variables, hidden),
            shape(table, hidden),
            shape(1, 1),
        ],
        (total, other, latent_grad, mean_loss),
        [pltpu.VMEM((variables, hidden), F32), pltpu.SemaphoreType.DMA((5,))],
        sink=HBM,
    )
    return (latent_out[None], proj_grad, coef_grad, loss_out.reshape(1))


def solution(mesh):
    placed = (
        P(("groups", "member"), "band", None),
        P(),
        P(),
        P(None, ("groups", "band")),
        P("band"),
        P(),
        P(),
        P(None, "band", None),
        P(),
    )
    return jax.shard_map(
        local,
        mesh=mesh,
        in_specs=placed,
        out_specs=(
            P(("groups", "member"), "band", None),
            P("groups", None),
            P("groups", None),
            P("groups"),
        ),
        check_vma=False,
    )
```

```python
import functools
import math

import jax
import jax.numpy as jnp
from jax import lax
from jax.experimental import pallas as pl
from jax.experimental.pallas import tpu as pltpu
from jax.sharding import PartitionSpec as P

K = 4
LANES = 128
FAIR_ALPHA = 0.95
SOFTNESS = 0.1
F32 = jnp.float32
BF16 = jnp.bfloat16
VMEM = pl.BlockSpec(memory_space=pltpu.VMEM)
HBM = pl.BlockSpec(memory_space=pltpu.HBM)
PARAMS = pltpu.CompilerParams(vmem_limit_bytes=24 * 1024 * 1024)


def swap(shard, axis, mask):
    peers = lax.axis_size(axis)
    return lax.ppermute(shard, axis, [(i, i ^ mask) for i in range(peers)])


def cross(shard, member_mask, band_mask):
    members, bands = lax.axis_size("member"), lax.axis_size("band")
    pairs = [
        (m * bands + b, (m ^ member_mask) * bands + (b ^ band_mask))
        for m in range(members)
        for b in range(bands)
    ]
    return lax.ppermute(shard, ("member", "band"), pairs)


def odd(value):
    return value.bit_count() & 1


def parity(index, peers):
    found = 0
    for bit in range(peers.bit_length() - 1):
        found = lax.bitwise_xor(found, lax.bitwise_and(lax.shift_right_logical(index, bit), 1))
    return found


def half_here(members, bands):
    return lax.bitwise_xor(parity(lax.axis_index("member"), members), parity(lax.axis_index("band"), bands))


def soft_abs(values):
    return jnp.sqrt(values * values + SOFTNESS * SOFTNESS) - SOFTNESS


def soft_slope(values):
    return values * lax.rsqrt(values * values + SOFTNESS * SOFTNESS)


def up(size, unit):
    return -(-size // unit) * unit


def dot(left, right, left_dim, right_dim):
    return lax.dot_general(
        left, right, (((left_dim,), (right_dim,)), ((), ())), preferred_element_type=F32
    )


def pieces_of(values):
    high = values.astype(BF16)
    rest = values - high.astype(F32)
    mid = rest.astype(BF16)
    low = (rest - mid.astype(F32)).astype(BF16)
    return high, mid, low


def parts(values):
    return jnp.concatenate(pieces_of(values), axis=0)


def whole(stacked):
    rows = stacked.shape[0] // 3
    return (stacked[:rows] + stacked[rows : 2 * rows]) + stacked[2 * rows :]


def hot(ids, size):
    rows = lax.broadcasted_iota(jnp.int32, (size, ids.shape[1]), 0)
    return jnp.where(rows == ids, 1.0, 0.0).astype(BF16)


def pick(table, ids):
    rows, size = table.shape
    slots = ids.shape[1]
    if slots % LANES or size % LANES:
        return [whole(dot(parts(table), hot(ids, size), 1, 0))]
    pieces = []
    for first in range(0, slots, LANES):
        chosen = jnp.broadcast_to(ids[:, first : first + LANES], (rows, LANES))
        lane = lax.rem(chosen, LANES)
        block = lax.div(chosen, LANES)
        found = jnp.zeros((rows, LANES), F32)
        for start in range(0, size, LANES):
            there = jnp.take_along_axis(table[:, start : start + LANES], lane, axis=1, mode="promise_in_bounds")
            found = jnp.where(block == start // LANES, there, found)
        pieces.append(found)
    return pieces


def packed_shape(variables, slots):
    pieces = slots // LANES if slots % LANES == 0 else 1
    return up(pieces * (variables + 1), 8), slots // pieces


def pack(payload, pieces, cells, variables):
    lanes = payload.shape[1]
    full = variables // 8 * 8
    base = len(pieces) * full
    payload[base:, :] = jnp.zeros((payload.shape[0] - base, lanes), F32)
    for n, piece in enumerate(pieces):
        payload[n * full : (n + 1) * full, :] = piece[0:full]
        row = base + n * (variables + 1 - full)
        payload[row : row + variables - full, :] = piece[full:variables]
        payload[row + variables - full : row + variables - full + 1, :] = cells[:, n * lanes : (n + 1) * lanes]


def unpack(payload, variables, slots):
    lanes = payload.shape[1]
    full = variables // 8 * 8
    base = slots // lanes * full
    values, cells = [], []
    for n in range(slots // lanes):
        row = base + n * (variables + 1 - full)
        piece = payload[n * full : (n + 1) * full, :]
        for extra in range(variables - full):
            here = lax.broadcasted_iota(jnp.int32, (8, lanes), 0) == extra
            one = jnp.where(here, payload[row + extra : row + extra + 1, :], 0.0)
            tail = one if extra == 0 else tail + one
        values.append(jnp.concatenate([piece, tail], axis=0) if variables > full else piece)
        cells.append(payload[row + variables - full : row + variables - full + 1, :])
    if len(values) == 1:
        return values[0], cells[0]
    return jnp.concatenate(values, axis=1), jnp.concatenate(cells, axis=1)


def project_kernel(*refs):
    (latent_in, coef_in, proj_in, source_in, weight_in, target_in, wanted_in, area_in, factor_in, *rest) = refs
    *payloads, proj, proj_pad, products, pair_ids, target, wanted, area, factor = rest[:-5]
    latent, coef, source, weight, arrivals = rest[-5:]
    moves = [
        pltpu.make_async_copy(there, here, arrivals.at[n])
        for n, (there, here) in enumerate(
            [
                (latent_in, latent),
                (coef_in, coef),
                (proj_in, proj),
                (source_in, source),
                (weight_in, weight),
                (target_in, target),
                (wanted_in, wanted),
                (area_in, area),
                (factor_in, factor),
            ]
        )
    ]
    for move in moves:
        move.start()
    bands = len(payloads)
    here = lax.axis_index("band")
    rows, hidden = latent.shape
    table = coef.shape[0]
    variables = proj.shape[0]
    proj_pad[...] = jnp.zeros_like(proj_pad)
    for move in moves[:3]:
        move.wait()
    proj_pad[0:variables, :] = proj[...]
    wide = latent[...].astype(F32)
    scale = coef[...].astype(F32)
    for q in range(table):
        products[q * rows : (q + 1) * rows, :] = (wide * scale[q : q + 1, :]).astype(BF16)
    projected = dot(proj_pad[...], products[...], 1, 1)
    for move in moves[3:]:
        move.wait()
    for i in range(bands):
        there = lax.bitwise_xor(here, i)
        ids = weight[here, pl.ds(there, 1), :] * rows + source[here, pl.ds(there, 1), :]
        pair_ids[i] = ids
        pack(payloads[i], pick(projected, ids), target[there, :, :].astype(F32), variables)


def predict_kernel(variables, *refs):
    *payloads, target, predicted = refs
    payloads = payloads[::-1]
    bands = len(payloads)
    here = lax.axis_index("band")
    total = 0.0
    for i in range(bands):
        there = lax.bitwise_xor(here, i)
        arrived, _ = unpack(payloads[i], variables, target.shape[2])
        total = total + dot(parts(arrived), hot(target[there, :, :], predicted.shape[1]), 1, 1)
    predicted[...] = whole(total)


def count_kernel(variables, cells_dev, pair_ids, *refs):
    *payloads, counts = refs
    payloads = payloads[::-1]
    for i, payload in enumerate(payloads):
        cells = unpack(payload, variables, pair_ids.shape[2])[1].astype(jnp.int32)
        block = dot(hot(pair_ids[i], counts.shape[0]), hot(cells, cells_dev), 1, 1)
        counts[:, i * cells_dev : (i + 1) * cells_dev] = block.astype(BF16)


def grade_kernel(pair_coef, target, area, var_weight, *refs):
    *predicted, grad, rows = refs
    members = len(predicted)
    here = lax.bitwise_xor(lax.axis_index("member"), 1)
    variables = target.shape[0]
    wanted = target[...]
    spots = lax.broadcasted_iota(jnp.int32, (variables, variables), 0)
    same = spots == lax.broadcasted_iota(jnp.int32, (variables, variables), 1)
    column = jnp.sum(jnp.where(same, var_weight[...], 0.0), axis=1, keepdims=True)
    weights = column * area[...]
    values = [ref[0:variables, :] for ref in predicted]
    own = values[0]
    slopes = 0.0
    for other in values[1:]:
        slopes = slopes + soft_slope(own - other)
    grad_pred = weights * (soft_slope(own - wanted) - pair_coef * slopes)
    for bit in range(members.bit_length() - 1):
        flip = lax.bitwise_and(lax.shift_right_logical(here, bit), 1) == 1
        ordered = list(values)
        for i in range(members):
            if not i >> bit & 1:
                first, second = values[i], values[i ^ (1 << bit)]
                ordered[i] = jnp.where(flip, second, first)
                ordered[i ^ (1 << bit)] = jnp.where(flip, first, second)
        values = ordered
    loss = 0.0
    spread = 0.0
    for m in range(members):
        loss = loss + soft_abs(values[m] - wanted)
        for k in range(m + 1, members):
            spread = spread + soft_abs(values[m] - values[k])
    total = jnp.sum(weights * (loss - pair_coef * spread), axis=(0, 1), keepdims=True)
    lane = lax.broadcasted_iota(jnp.int32, rows.shape, 1)
    pieces = [piece.astype(F32) for piece in pieces_of(total)]
    rows[...] = jnp.where(lane == 0, pieces[0], jnp.where(lane == 1, pieces[1], jnp.where(lane == 2, pieces[2], 0.0)))
    rows[0:variables, :] = grad_pred
    grad[...] = rows[...].astype(BF16)


def back_to_pairs(grad, proj, counts):
    return dot(grad, proj, 0, 0).astype(BF16), dot(grad, counts, 1, 1)


def only_grads(arrived, variables):
    row = lax.broadcasted_iota(jnp.int32, arrived.shape, 0)
    return jnp.where(row < variables, arrived.astype(F32), 0.0).astype(BF16)


def early_kernel(index, variables, proj, counts, grad, *refs):
    *before, pair_grad, block, cell_grad = refs
    cells_dev = grad.shape[1]
    own = counts[:, index * cells_dev : (index + 1) * cells_dev]
    cell_grad[...], pairs_here = back_to_pairs(only_grads(grad[...], variables), proj[...], own)
    pair_grad[...] = before[0][...] + pairs_here if before else pairs_here
    step = 256
    for h in range(0, block.shape[1], step):
        here = dot(own, cell_grad[:, h : h + step], 1, 0)
        block[:, h : h + step] = before[1][:, h : h + step] + here if before else here


def backward_kernel(members, variables, early, scale_proj, scale_coef, scale_loss, latent, coef, proj, counts, products, *refs):
    near_pair_grad, near_block, *grads = refs[:-6]
    latent_grad, keep, send, mean_loss, cell_grad, sums = refs[-6:]
    bands = len(grads)
    band = lax.axis_index("band")
    side = half_here(members, bands)
    rows, hidden = latent.shape
    table = coef.shape[0]
    cells_dev = grads[0].shape[1]
    padded = grads[0].shape[0]
    lane = lax.broadcasted_iota(jnp.int32, (1, 128), 1)
    losses = jnp.zeros((1, 128), F32)
    pair_grad = near_pair_grad[...]
    for i in range(bands):
        there = lax.bitwise_xor(band, i)
        arrived = grads[i][...].astype(F32)
        loss = jnp.sum(arrived[variables : variables + 1, 0:128], axis=1, keepdims=True)
        losses = losses + jnp.where(lane == there, loss, 0.0)
        if i not in early:
            spot = slice((i - 1) * cells_dev, i * cells_dev)
            cell_grad[spot, :], here = back_to_pairs(
                only_grads(grads[i][...], variables),
                proj[...],
                counts[:, i * cells_dev : (i + 1) * cells_dev],
            )
            pair_grad = pair_grad + here
    mean_loss[...] = jnp.sum(losses, axis=1, keepdims=True) * scale_loss
    sums[0:padded, :] = whole(dot(parts(pair_grad), products[...], 1, 0)) * scale_proj
    step = 256
    for h in range(0, hidden, step):
        block = near_block[:, h : h + step] + dot(counts[:, cells_dev : cells_dev + cell_grad.shape[0]], cell_grad[:, h : h + step], 1, 0)
        wide = latent[:, h : h + step].astype(F32)
        scale = coef[:, h : h + step].astype(F32)
        into_latent = 0.0
        for q in range(table):
            piece = block[q * rows : (q + 1) * rows, :]
            into_latent = into_latent + piece * scale[q : q + 1, :]
            sums[padded + q : padded + q + 1, h : h + step] = (
                jnp.sum(piece * wide, axis=0, keepdims=True) * scale_coef
            )
        latent_grad[:, h : h + step] = into_latent.astype(BF16)
    half = hidden // 2
    left, right = sums[:, 0:half], sums[:, half:hidden]
    keep[...] = jnp.where(side == 0, left, right)
    send[...] = jnp.where(side == 0, right, left)


def write_kernel(members, bands, variables, scaled, other, latent_grad, mean_loss, *refs):
    latent_out, proj_out, coef_out, loss_out, proj, leaves = refs
    side = half_here(members, bands)
    half = scaled.shape[1]
    first = scaled.shape[0] - coef_out.shape[0]
    here = pl.ds(pl.multiple_of(side * half, half), half)
    there = pl.ds(pl.multiple_of((1 - side) * half, half), half)
    moves = [
        (scaled.at[first:, :], coef_out.at[:, here]),
        (other.at[first:, :], coef_out.at[:, there]),
        (latent_grad, latent_out),
        (mean_loss, loss_out),
        (proj, proj_out),
    ]
    moves = [pltpu.make_async_copy(*move, leaves.at[n]) for n, move in enumerate(moves)]
    for move in moves[:-1]:
        move.start()
    mine, theirs = scaled[0:variables, :], other[0:variables, :]
    proj[:, 0:half] = jnp.where(side == 0, mine, theirs)
    proj[:, half:] = jnp.where(side == 0, theirs, mine)
    moves[-1].start()
    for move in moves:
        move.wait()


def call(kernel, outs, operands, scratch=(), flops=0, source=VMEM, sink=VMEM):
    if source is HBM:
        operands = [pltpu.with_memory_space_constraint(x, pltpu.HBM) for x in operands]
    return pl.pallas_call(
        kernel,
        out_shape=outs,
        in_specs=[source] * len(operands),
        out_specs=[sink] * len(outs),
        scratch_shapes=list(scratch),
        compiler_params=PARAMS,
        cost_estimate=pl.CostEstimate(flops=flops, bytes_accessed=1 << 20, transcendentals=0),
    )(*operands)


def shape(*dims, dtype=F32):
    return jax.ShapeDtypeStruct(dims, dtype)


def local(
    latent,
    coef_table,
    out_proj,
    target,
    cell_area,
    var_weight,
    edge_source,
    edge_target,
    edge_weight,
):
    latent_rows = latent[0]
    rows, hidden = latent_rows.shape
    bands = lax.axis_size("band")
    members = lax.axis_size("member")
    variables, cells_dev = target.shape
    cells_all = cells_dev * bands
    table = coef_table.shape[0]
    slots = edge_source.shape[2]
    pairs = table * rows
    padded = up(variables + 1, 16)
    pair_coef = FAIR_ALPHA / (members - 1) + (1.0 - FAIR_ALPHA) / members

    *payloads, _, proj_pad, products, pair_ids, cell_ids, wanted, area, factor = call(
        project_kernel,
        [shape(*packed_shape(variables, slots))] * bands
        + [
            shape(variables, hidden, dtype=BF16),
            shape(padded, hidden, dtype=BF16),
            shape(pairs, hidden, dtype=BF16),
            shape(bands, 1, slots, dtype=jnp.int32),
            shape(bands, 1, slots, dtype=jnp.int32),
            shape(variables, cells_dev),
            shape(1, cells_dev),
            shape(1, variables),
        ],
        (
            latent_rows,
            coef_table,
            out_proj,
            edge_source,
            edge_weight,
            edge_target,
            target,
            cell_area.reshape(1, -1),
            var_weight.reshape(1, -1),
        ),
        [
            pltpu.VMEM((rows, hidden), BF16),
            pltpu.VMEM((table, hidden), BF16),
            pltpu.VMEM(edge_source.shape, jnp.int32),
            pltpu.VMEM(edge_weight.shape, jnp.int32),
            pltpu.SemaphoreType.DMA((9,)),
        ],
        source=HBM,
    )
    arrived = [cross(payloads[i], 1, i) for i in range(bands)][::-1]
    (predicted,) = call(
        functools.partial(predict_kernel, variables),
        [shape(up(variables, 8), cells_dev)],
        (*arrived, cell_ids),
    )
    (counts,) = call(
        functools.partial(count_kernel, variables, cells_dev),
        [shape(pairs, cells_all, dtype=BF16)],
        (pair_ids, *arrived),
        flops=2 * pairs * slots * cells_all,
    )
    members_here = [predicted, swap(predicted, "member", 1)]
    for i in range(2, members, 2):
        far = cross(predicted, i + 1, 0)
        if i == 2:
            far, counts = lax.optimization_barrier((far, counts))
        members_here += [swap(far, "member", 1), far]
    (grad,) = call(
        functools.partial(grade_kernel, pair_coef),
        [shape(padded, cells_dev, dtype=BF16)],
        (wanted, area, factor, *members_here),
        [pltpu.VMEM((padded, cells_dev), F32)],
    )
    grads = [cross(grad, 1, i) for i in range(bands)]
    early = sorted({0, bands - 1})
    sums = ()
    for index in early:
        sums = call(
            functools.partial(early_kernel, index, variables),
            [shape(padded, pairs), shape(pairs, hidden)],
            (proj_pad, counts, grads[index], *sums),
            [pltpu.VMEM((cells_dev, hidden), BF16)],
            flops=2 * pairs * cells_dev * hidden,
        )
    latent_grad, keep, send, mean_loss = call(
        functools.partial(
            backward_kernel,
            members,
            variables,
            early,
            1.0 / math.sqrt(members * cells_all),
            1.0 / math.sqrt(members * cells_all * K),
            1.0 / (members * variables * cells_all),
        ),
        [
            shape(rows, hidden, dtype=BF16),
            shape(padded + table, hidden // 2),
            shape(padded + table, hidden // 2),
            shape(1, 1),
        ],
        (latent_rows, coef_table, proj_pad, counts, products, *sums, *grads),
        [
            pltpu.VMEM((cells_all - len(early) * cells_dev, hidden), BF16),
            pltpu.VMEM((padded + table, hidden), F32),
        ],
    )
    total = keep + swap(send, "member", 1)
    step = 2
    while step < members:
        rounded = total.astype(BF16)
        total = rounded.astype(F32) + cross(rounded, step + 1, 0).astype(F32)
        step *= 2
    step = 1
    while step < bands:
        rounded = total.astype(BF16)
        total = rounded.astype(F32) + cross(rounded, odd(step), step).astype(F32)
        if 2 * step < bands:
            far = [cross(rounded, odd(step * k), step * k).astype(F32) for k in (2, 3)]
            total = total + (far[0] + far[1])
        step *= 4
    other = swap(total, "member", 1)
    latent_out, proj_grad, coef_grad, loss_out = call(
        functools.partial(write_kernel, members, bands, variables),
        [
            shape(rows, hidden, dtype=BF16),
            shape(variables, hidden),
            shape(table, hidden),
            shape(1, 1),
        ],
        (total, other, latent_grad, mean_loss),
        [pltpu.VMEM((variables, hidden), F32), pltpu.SemaphoreType.DMA((5,))],
        sink=HBM,
    )
    return (latent_out[None], proj_grad, coef_grad, loss_out.reshape(1))


def solution(mesh):
    placed = (
        P(("groups", "member"), "band", None),
        P(),
        P(),
        P(None, ("groups", "band")),
        P("band"),
        P(),
        P(),
        P(None, "band", None),
        P(),
    )
    return jax.shard_map(
        local,
        mesh=mesh,
        in_specs=placed,
        out_specs=(
            P(("groups", "member"), "band", None),
            P("groups", None),
            P("groups", None),
            P("groups"),
        ),
        check_vma=False,
    )
```

```python
import functools
import math

import jax
import jax.numpy as jnp
from jax import lax
from jax.experimental import pallas as pl
from jax.experimental.pallas import tpu as pltpu
from jax.sharding import PartitionSpec as P

K = 4
LANES = 128
FAIR_ALPHA = 0.95
SOFTNESS = 0.1
F32 = jnp.float32
BF16 = jnp.bfloat16
VMEM = pl.BlockSpec(memory_space=pltpu.VMEM)
HBM = pl.BlockSpec(memory_space=pltpu.HBM)
PARAMS = pltpu.CompilerParams(vmem_limit_bytes=24 * 1024 * 1024)


def swap(shard, axis, mask):
    peers = lax.axis_size(axis)
    return lax.ppermute(shard, axis, [(i, i ^ mask) for i in range(peers)])


def cross(shard, member_mask, band_mask):
    members, bands = lax.axis_size("member"), lax.axis_size("band")
    pairs = [
        (m * bands + b, (m ^ member_mask) * bands + (b ^ band_mask))
        for m in range(members)
        for b in range(bands)
    ]
    return lax.ppermute(shard, ("member", "band"), pairs)


def odd(value):
    return value.bit_count() & 1


def parity(index, peers):
    found = 0
    for bit in range(peers.bit_length() - 1):
        found = lax.bitwise_xor(found, lax.bitwise_and(lax.shift_right_logical(index, bit), 1))
    return found


def half_here(members, bands):
    return lax.bitwise_xor(parity(lax.axis_index("member"), members), parity(lax.axis_index("band"), bands))


def soft_abs(values):
    return jnp.sqrt(values * values + SOFTNESS * SOFTNESS) - SOFTNESS


def soft_slope(values):
    return values * lax.rsqrt(values * values + SOFTNESS * SOFTNESS)


def up(size, unit):
    return -(-size // unit) * unit


def dot(left, right, left_dim, right_dim):
    return lax.dot_general(
        left, right, (((left_dim,), (right_dim,)), ((), ())), preferred_element_type=F32
    )


def pieces_of(values):
    high = values.astype(BF16)
    rest = values - high.astype(F32)
    mid = rest.astype(BF16)
    low = (rest - mid.astype(F32)).astype(BF16)
    return high, mid, low


def parts(values):
    return jnp.concatenate(pieces_of(values), axis=0)


def whole(stacked):
    rows = stacked.shape[0] // 3
    return (stacked[:rows] + stacked[rows : 2 * rows]) + stacked[2 * rows :]


def hot(ids, size):
    rows = lax.broadcasted_iota(jnp.int32, (size, ids.shape[1]), 0)
    return jnp.where(rows == ids, 1.0, 0.0).astype(BF16)


def pick(table, ids):
    rows, size = table.shape
    slots = ids.shape[1]
    if slots % LANES or size % LANES:
        return [whole(dot(parts(table), hot(ids, size), 1, 0))]
    pieces = []
    for first in range(0, slots, LANES):
        chosen = jnp.broadcast_to(ids[:, first : first + LANES], (rows, LANES))
        lane = lax.rem(chosen, LANES)
        block = lax.div(chosen, LANES)
        found = jnp.zeros((rows, LANES), F32)
        for start in range(0, size, LANES):
            there = jnp.take_along_axis(table[:, start : start + LANES], lane, axis=1, mode="promise_in_bounds")
            found = jnp.where(block == start // LANES, there, found)
        pieces.append(found)
    return pieces


def packed_shape(variables, slots):
    pieces = slots // LANES if slots % LANES == 0 else 1
    return up(pieces * (variables + 1), 8), slots // pieces


def pack(payload, pieces, cells, variables):
    lanes = payload.shape[1]
    full = variables // 8 * 8
    base = len(pieces) * full
    payload[base:, :] = jnp.zeros((payload.shape[0] - base, lanes), F32)
    for n, piece in enumerate(pieces):
        payload[n * full : (n + 1) * full, :] = piece[0:full]
        row = base + n * (variables + 1 - full)
        payload[row : row + variables - full, :] = piece[full:variables]
        payload[row + variables - full : row + variables - full + 1, :] = cells[:, n * lanes : (n + 1) * lanes]


def unpack(payload, variables, slots):
    lanes = payload.shape[1]
    full = variables // 8 * 8
    base = slots // lanes * full
    values, cells = [], []
    for n in range(slots // lanes):
        row = base + n * (variables + 1 - full)
        piece = payload[n * full : (n + 1) * full, :]
        for extra in range(variables - full):
            here = lax.broadcasted_iota(jnp.int32, (8, lanes), 0) == extra
            one = jnp.where(here, payload[row + extra : row + extra + 1, :], 0.0)
            tail = one if extra == 0 else tail + one
        values.append(jnp.concatenate([piece, tail], axis=0) if variables > full else piece)
        cells.append(payload[row + variables - full : row + variables - full + 1, :])
    if len(values) == 1:
        return values[0], cells[0]
    return jnp.concatenate(values, axis=1), jnp.concatenate(cells, axis=1)


def project_kernel(*refs):
    (latent_in, coef_in, proj_in, source_in, weight_in, target_in, wanted_in, area_in, factor_in, *rest) = refs
    *payloads, proj, proj_pad, products, pair_ids, target, wanted, area, factor = rest[:-5]
    latent, coef, source, weight, arrivals = rest[-5:]
    moves = [
        pltpu.make_async_copy(there, here, arrivals.at[n])
        for n, (there, here) in enumerate(
            [
                (latent_in, latent),
                (coef_in, coef),
                (proj_in, proj),
                (source_in, source),
                (weight_in, weight),
                (target_in, target),
                (wanted_in, wanted),
                (area_in, area),
                (factor_in, factor),
            ]
        )
    ]
    for move in moves:
        move.start()
    bands = len(payloads)
    here = lax.axis_index("band")
    rows, hidden = latent.shape
    table = coef.shape[0]
    variables = proj.shape[0]
    proj_pad[...] = jnp.zeros_like(proj_pad)
    for move in moves[:3]:
        move.wait()
    proj_pad[0:variables, :] = proj[...]
    wide = latent[...].astype(F32)
    scale = coef[...].astype(F32)
    for q in range(table):
        products[q * rows : (q + 1) * rows, :] = (wide * scale[q : q + 1, :]).astype(BF16)
    projected = dot(proj_pad[...], products[...], 1, 1)
    for move in moves[3:]:
        move.wait()
    for i in range(bands):
        there = lax.bitwise_xor(here, i)
        ids = weight[here, pl.ds(there, 1), :] * rows + source[here, pl.ds(there, 1), :]
        pair_ids[i] = ids
        pack(payloads[i], pick(projected, ids), target[there, :, :].astype(F32), variables)


def predict_kernel(variables, *refs):
    *payloads, target, predicted = refs
    payloads = payloads[::-1]
    bands = len(payloads)
    here = lax.axis_index("band")
    total = 0.0
    for i in range(bands):
        there = lax.bitwise_xor(here, i)
        arrived, _ = unpack(payloads[i], variables, target.shape[2])
        total = total + dot(parts(arrived), hot(target[there, :, :], predicted.shape[1]), 1, 1)
    predicted[...] = whole(total)


def count_kernel(variables, cells_dev, pair_ids, *refs):
    *payloads, counts = refs
    payloads = payloads[::-1]
    for i, payload in enumerate(payloads):
        cells = unpack(payload, variables, pair_ids.shape[2])[1].astype(jnp.int32)
        block = dot(hot(pair_ids[i], counts.shape[0]), hot(cells, cells_dev), 1, 1)
        counts[:, i * cells_dev : (i + 1) * cells_dev] = block.astype(BF16)


def grade_kernel(pair_coef, target, area, var_weight, *refs):
    *predicted, grad, rows = refs
    members = len(predicted)
    here = lax.bitwise_xor(lax.axis_index("member"), 1)
    variables = target.shape[0]
    wanted = target[...]
    spots = lax.broadcasted_iota(jnp.int32, (variables, variables), 0)
    same = spots == lax.broadcasted_iota(jnp.int32, (variables, variables), 1)
    column = jnp.sum(jnp.where(same, var_weight[...], 0.0), axis=1, keepdims=True)
    weights = column * area[...]
    values = [ref[0:variables, :] for ref in predicted]
    own = values[0]
    slopes = 0.0
    for other in values[1:]:
        slopes = slopes + soft_slope(own - other)
    grad_pred = weights * (soft_slope(own - wanted) - pair_coef * slopes)
    for bit in range(members.bit_length() - 1):
        flip = lax.bitwise_and(lax.shift_right_logical(here, bit), 1) == 1
        ordered = list(values)
        for i in range(members):
            if not i >> bit & 1:
                first, second = values[i], values[i ^ (1 << bit)]
                ordered[i] = jnp.where(flip, second, first)
                ordered[i ^ (1 << bit)] = jnp.where(flip, first, second)
        values = ordered
    loss = 0.0
    spread = 0.0
    for m in range(members):
        loss = loss + soft_abs(values[m] - wanted)
        for k in range(m + 1, members):
            spread = spread + soft_abs(values[m] - values[k])
    total = jnp.sum(weights * (loss - pair_coef * spread), axis=(0, 1), keepdims=True)
    lane = lax.broadcasted_iota(jnp.int32, rows.shape, 1)
    pieces = [piece.astype(F32) for piece in pieces_of(total)]
    rows[...] = jnp.where(lane == 0, pieces[0], jnp.where(lane == 1, pieces[1], jnp.where(lane == 2, pieces[2], 0.0)))
    rows[0:variables, :] = grad_pred
    grad[...] = rows[...].astype(BF16)


def back_to_pairs(grad, proj, counts):
    return dot(grad, proj, 0, 0).astype(BF16), dot(grad, counts, 1, 1)


def only_grads(arrived, variables):
    row = lax.broadcasted_iota(jnp.int32, arrived.shape, 0)
    return jnp.where(row < variables, arrived.astype(F32), 0.0).astype(BF16)


def early_kernel(index, variables, proj, counts, grad, *refs):
    *before, pair_grad, block, cell_grad = refs
    cells_dev = grad.shape[1]
    own = counts[:, index * cells_dev : (index + 1) * cells_dev]
    cell_grad[...], pairs_here = back_to_pairs(only_grads(grad[...], variables), proj[...], own)
    pair_grad[...] = before[0][...] + pairs_here if before else pairs_here
    step = 256
    for h in range(0, block.shape[1], step):
        here = dot(own, cell_grad[:, h : h + step], 1, 0)
        block[:, h : h + step] = before[1][:, h : h + step] + here if before else here


def backward_kernel(members, variables, early, sent, scales, latent, coef, proj, counts, products, *refs):
    near_pair_grad, near_block, *rest = refs
    bands = lax.axis_size("band")
    grads, rest = rest[:bands], rest[bands:]
    latent_grad, sums, *all_pairs, cell_grad, wide_pairs = rest
    scale_proj, scale_coef = scales
    side = half_here(members, bands)
    rows, half = latent_grad.shape
    table = coef.shape[0]
    cells_dev = grads[0].shape[1]
    padded = grads[0].shape[0]
    base = (1 - side if sent else side) * half
    here = pl.ds(pl.multiple_of(base, half), half)
    wide_pairs[...] = near_pair_grad[...]
    for i in range(bands):
        if i not in early:
            grad = only_grads(grads[i][...], variables)
            spot = slice((i - 1) * cells_dev, i * cells_dev)
            cell_grad[spot, :] = dot(grad, proj[:, here], 0, 0).astype(BF16)
            if sent:
                wide_pairs[...] += dot(grad, counts[:, i * cells_dev : (i + 1) * cells_dev], 1, 1)
    if sent:
        all_pairs[0][...] = wide_pairs[...]
    sums[0:padded, :] = whole(dot(parts(wide_pairs[...]), products[:, here], 1, 0)) * scale_proj
    step = 256
    for h in range(0, half, step):
        spot = pl.ds(pl.multiple_of(base + h, step), step)
        block = near_block[:, spot] + dot(
            counts[:, cells_dev : cells_dev + cell_grad.shape[0]], cell_grad[:, h : h + step], 1, 0
        )
        wide = latent[:, spot].astype(F32)
        scale = coef[:, spot].astype(F32)
        into_latent = 0.0
        for q in range(table):
            piece = block[q * rows : (q + 1) * rows, :]
            into_latent = into_latent + piece * scale[q : q + 1, :]
            sums[padded + q : padded + q + 1, h : h + step] = (
                jnp.sum(piece * wide, axis=0, keepdims=True) * scale_coef
            )
        latent_grad[:, h : h + step] = into_latent.astype(BF16)


def loss_kernel(variables, scale, *refs):
    *grads, mean_loss = refs
    band = lax.axis_index("band")
    lane = lax.broadcasted_iota(jnp.int32, (1, 128), 1)
    losses = jnp.zeros((1, 128), F32)
    for i, grad in enumerate(grads):
        arrived = grad[...].astype(F32)
        loss = jnp.sum(arrived[variables : variables + 1, 0:128], axis=1, keepdims=True)
        losses = losses + jnp.where(lane == lax.bitwise_xor(band, i), loss, 0.0)
    mean_loss[...] = jnp.sum(losses, axis=1, keepdims=True) * scale


def write_kernel(members, bands, variables, scaled, other, latent_here, latent_there, mean_loss, *refs):
    latent_out, proj_out, coef_out, loss_out, proj, leaves = refs
    side = half_here(members, bands)
    half = scaled.shape[1]
    first = scaled.shape[0] - coef_out.shape[0]
    here = pl.ds(pl.multiple_of(side * half, half), half)
    there = pl.ds(pl.multiple_of((1 - side) * half, half), half)
    moves = [
        (scaled.at[first:, :], coef_out.at[:, here]),
        (other.at[first:, :], coef_out.at[:, there]),
        (latent_here, latent_out.at[:, here]),
        (latent_there, latent_out.at[:, there]),
        (mean_loss, loss_out),
        (proj, proj_out),
    ]
    moves = [pltpu.make_async_copy(*move, leaves.at[n]) for n, move in enumerate(moves)]
    for move in moves[:-1]:
        move.start()
    mine, theirs = scaled[0:variables, :], other[0:variables, :]
    proj[:, 0:half] = jnp.where(side == 0, mine, theirs)
    proj[:, half:] = jnp.where(side == 0, theirs, mine)
    moves[-1].start()
    for move in moves:
        move.wait()


def call(kernel, outs, operands, scratch=(), flops=0, source=VMEM, sink=VMEM):
    if source is HBM:
        operands = [pltpu.with_memory_space_constraint(x, pltpu.HBM) for x in operands]
    return pl.pallas_call(
        kernel,
        out_shape=outs,
        in_specs=[source] * len(operands),
        out_specs=[sink] * len(outs),
        scratch_shapes=list(scratch),
        compiler_params=PARAMS,
        cost_estimate=pl.CostEstimate(flops=flops, bytes_accessed=1 << 20, transcendentals=0),
    )(*operands)


def shape(*dims, dtype=F32):
    return jax.ShapeDtypeStruct(dims, dtype)


def local(
    latent,
    coef_table,
    out_proj,
    target,
    cell_area,
    var_weight,
    edge_source,
    edge_target,
    edge_weight,
):
    latent_rows = latent[0]
    rows, hidden = latent_rows.shape
    bands = lax.axis_size("band")
    members = lax.axis_size("member")
    variables, cells_dev = target.shape
    cells_all = cells_dev * bands
    table = coef_table.shape[0]
    slots = edge_source.shape[2]
    pairs = table * rows
    padded = up(variables + 1, 16)
    pair_coef = FAIR_ALPHA / (members - 1) + (1.0 - FAIR_ALPHA) / members

    *payloads, _, proj_pad, products, pair_ids, cell_ids, wanted, area, factor = call(
        project_kernel,
        [shape(*packed_shape(variables, slots))] * bands
        + [
            shape(variables, hidden, dtype=BF16),
            shape(padded, hidden, dtype=BF16),
            shape(pairs, hidden, dtype=BF16),
            shape(bands, 1, slots, dtype=jnp.int32),
            shape(bands, 1, slots, dtype=jnp.int32),
            shape(variables, cells_dev),
            shape(1, cells_dev),
            shape(1, variables),
        ],
        (
            latent_rows,
            coef_table,
            out_proj,
            edge_source,
            edge_weight,
            edge_target,
            target,
            cell_area.reshape(1, -1),
            var_weight.reshape(1, -1),
        ),
        [
            pltpu.VMEM((rows, hidden), BF16),
            pltpu.VMEM((table, hidden), BF16),
            pltpu.VMEM(edge_source.shape, jnp.int32),
            pltpu.VMEM(edge_weight.shape, jnp.int32),
            pltpu.SemaphoreType.DMA((9,)),
        ],
        source=HBM,
    )
    arrived = [cross(payloads[i], 1, i) for i in range(bands)][::-1]
    (predicted,) = call(
        functools.partial(predict_kernel, variables),
        [shape(up(variables, 8), cells_dev)],
        (*arrived, cell_ids),
    )
    (counts,) = call(
        functools.partial(count_kernel, variables, cells_dev),
        [shape(pairs, cells_all, dtype=BF16)],
        (pair_ids, *arrived),
        flops=2 * pairs * slots * cells_all,
    )
    members_here = [predicted, swap(predicted, "member", 1)]
    for i in range(2, members, 2):
        far = cross(predicted, i + 1, 0)
        if i == 2:
            far, counts = lax.optimization_barrier((far, counts))
        members_here += [swap(far, "member", 1), far]
    (grad,) = call(
        functools.partial(grade_kernel, pair_coef),
        [shape(padded, cells_dev, dtype=BF16)],
        (wanted, area, factor, *members_here),
        [pltpu.VMEM((padded, cells_dev), F32)],
    )
    grads = [cross(grad, 1, i) for i in range(bands)]
    early = sorted({0, bands - 1})
    sums = ()
    for index in early:
        sums = call(
            functools.partial(early_kernel, index, variables),
            [shape(padded, pairs), shape(pairs, hidden)],
            (proj_pad, counts, grads[index], *sums),
            [pltpu.VMEM((cells_dev, hidden), BF16)],
            flops=2 * pairs * cells_dev * hidden,
        )
    half = hidden // 2
    scales = (
        1.0 / math.sqrt(members * cells_all),
        1.0 / math.sqrt(members * cells_all * K),
    )
    pair_grad, block = sums

    def half_back(sent, pair_grad):
        return call(
            functools.partial(backward_kernel, members, variables, early, sent, scales),
            [shape(rows, half, dtype=BF16), shape(padded + table, half)] + [shape(padded, pairs)] * sent,
            (latent_rows, coef_table, proj_pad, counts, products, pair_grad, block, *grads),
            [
                pltpu.VMEM((cells_all - len(early) * cells_dev, half), BF16),
                pltpu.VMEM((padded, pairs), F32),
            ],
            flops=2 * pairs * cells_all * half,
        )

    latent_there, send, pair_grad = half_back(True, pair_grad)
    latent_here, keep = half_back(False, pair_grad)
    (mean_loss,) = call(
        functools.partial(loss_kernel, variables, 1.0 / (members * variables * cells_all)),
        [shape(1, 1)],
        grads,
    )
    total = keep + swap(send, "member", 1)
    step = 2
    while step < members:
        rounded = total.astype(BF16)
        far = cross(rounded, step + 1, 0)
        if step == 2:
            far, mean_loss = lax.optimization_barrier((far, mean_loss))
        total = rounded.astype(F32) + far.astype(F32)
        step *= 2
    step = 1
    while step < bands:
        rounded = total.astype(BF16)
        total = rounded.astype(F32) + cross(rounded, odd(step), step).astype(F32)
        if 2 * step < bands:
            far = [cross(rounded, odd(step * k), step * k).astype(F32) for k in (2, 3)]
            total = total + (far[0] + far[1])
        step *= 4
    other = swap(total, "member", 1)
    latent_out, proj_grad, coef_grad, loss_out = call(
        functools.partial(write_kernel, members, bands, variables),
        [
            shape(rows, hidden, dtype=BF16),
            shape(variables, hidden),
            shape(table, hidden),
            shape(1, 1),
        ],
        (total, other, latent_here, latent_there, mean_loss),
        [pltpu.VMEM((variables, hidden), F32), pltpu.SemaphoreType.DMA((6,))],
        sink=HBM,
    )
    return (latent_out[None], proj_grad, coef_grad, loss_out.reshape(1))


def solution(mesh):
    placed = (
        P(("groups", "member"), "band", None),
        P(),
        P(),
        P(None, ("groups", "band")),
        P("band"),
        P(),
        P(),
        P(None, "band", None),
        P(),
    )
    return jax.shard_map(
        local,
        mesh=mesh,
        in_specs=placed,
        out_specs=(
            P(("groups", "member"), "band", None),
            P("groups", None),
            P("groups", None),
            P("groups"),
        ),
        check_vma=False,
    )
```

```python
import functools
import math

import jax
import jax.numpy as jnp
from jax import lax
from jax.experimental import pallas as pl
from jax.experimental.pallas import tpu as pltpu
from jax.sharding import PartitionSpec as P

K = 4
LANES = 128
FAIR_ALPHA = 0.95
SOFTNESS = 0.1
F32 = jnp.float32
BF16 = jnp.bfloat16
VMEM = pl.BlockSpec(memory_space=pltpu.VMEM)
HBM = pl.BlockSpec(memory_space=pltpu.HBM)
PARAMS = pltpu.CompilerParams(vmem_limit_bytes=24 * 1024 * 1024)


def swap(shard, axis, mask):
    peers = lax.axis_size(axis)
    return lax.ppermute(shard, axis, [(i, i ^ mask) for i in range(peers)])


def cross(shard, member_mask, band_mask):
    members, bands = lax.axis_size("member"), lax.axis_size("band")
    pairs = [
        (m * bands + b, (m ^ member_mask) * bands + (b ^ band_mask))
        for m in range(members)
        for b in range(bands)
    ]
    return lax.ppermute(shard, ("member", "band"), pairs)


def odd(value):
    return value.bit_count() & 1


def parity(index, peers):
    found = 0
    for bit in range(peers.bit_length() - 1):
        found = lax.bitwise_xor(found, lax.bitwise_and(lax.shift_right_logical(index, bit), 1))
    return found


def half_here(members, bands):
    return lax.bitwise_xor(parity(lax.axis_index("member"), members), parity(lax.axis_index("band"), bands))


def soft_abs(values):
    return jnp.sqrt(values * values + SOFTNESS * SOFTNESS) - SOFTNESS


def soft_slope(values):
    return values * lax.rsqrt(values * values + SOFTNESS * SOFTNESS)


def up(size, unit):
    return -(-size // unit) * unit


def dot(left, right, left_dim, right_dim):
    return lax.dot_general(
        left, right, (((left_dim,), (right_dim,)), ((), ())), preferred_element_type=F32
    )


def pieces_of(values):
    high = values.astype(BF16)
    rest = values - high.astype(F32)
    mid = rest.astype(BF16)
    low = (rest - mid.astype(F32)).astype(BF16)
    return high, mid, low


def parts(values):
    return jnp.concatenate(pieces_of(values), axis=0)


def whole(stacked):
    rows = stacked.shape[0] // 3
    return (stacked[:rows] + stacked[rows : 2 * rows]) + stacked[2 * rows :]


def hot(ids, size):
    rows = lax.broadcasted_iota(jnp.int32, (size, ids.shape[1]), 0)
    return jnp.where(rows == ids, 1.0, 0.0).astype(BF16)


def pick(table, ids):
    rows, size = table.shape
    slots = ids.shape[1]
    if slots % LANES or size % LANES:
        return [whole(dot(parts(table), hot(ids, size), 1, 0))]
    pieces = []
    for first in range(0, slots, LANES):
        chosen = jnp.broadcast_to(ids[:, first : first + LANES], (rows, LANES))
        lane = lax.rem(chosen, LANES)
        block = lax.div(chosen, LANES)
        found = jnp.zeros((rows, LANES), F32)
        for start in range(0, size, LANES):
            there = jnp.take_along_axis(table[:, start : start + LANES], lane, axis=1, mode="promise_in_bounds")
            found = jnp.where(block == start // LANES, there, found)
        pieces.append(found)
    return pieces


def packed_shape(variables, slots):
    pieces = slots // LANES if slots % LANES == 0 else 1
    return up(pieces * (variables + 1), 8), slots // pieces


def pack(payload, pieces, cells, variables):
    lanes = payload.shape[1]
    full = variables // 8 * 8
    base = len(pieces) * full
    payload[base:, :] = jnp.zeros((payload.shape[0] - base, lanes), F32)
    for n, piece in enumerate(pieces):
        payload[n * full : (n + 1) * full, :] = piece[0:full]
        row = base + n * (variables + 1 - full)
        payload[row : row + variables - full, :] = piece[full:variables]
        payload[row + variables - full : row + variables - full + 1, :] = cells[:, n * lanes : (n + 1) * lanes]


def unpack(payload, variables, slots):
    lanes = payload.shape[1]
    full = variables // 8 * 8
    base = slots // lanes * full
    values, cells = [], []
    for n in range(slots // lanes):
        row = base + n * (variables + 1 - full)
        piece = payload[n * full : (n + 1) * full, :]
        for extra in range(variables - full):
            here = lax.broadcasted_iota(jnp.int32, (8, lanes), 0) == extra
            one = jnp.where(here, payload[row + extra : row + extra + 1, :], 0.0)
            tail = one if extra == 0 else tail + one
        values.append(jnp.concatenate([piece, tail], axis=0) if variables > full else piece)
        cells.append(payload[row + variables - full : row + variables - full + 1, :])
    if len(values) == 1:
        return values[0], cells[0]
    return jnp.concatenate(values, axis=1), jnp.concatenate(cells, axis=1)


def project_kernel(*refs):
    (latent_in, coef_in, proj_in, source_in, weight_in, target_in, wanted_in, area_in, factor_in, *rest) = refs
    *payloads, proj, proj_pad, products, pair_ids, target, wanted, area, factor = rest[:-5]
    latent, coef, source, weight, arrivals = rest[-5:]
    moves = [
        pltpu.make_async_copy(there, here, arrivals.at[n])
        for n, (there, here) in enumerate(
            [
                (latent_in, latent),
                (coef_in, coef),
                (proj_in, proj),
                (source_in, source),
                (weight_in, weight),
                (target_in, target),
                (wanted_in, wanted),
                (area_in, area),
                (factor_in, factor),
            ]
        )
    ]
    for move in moves:
        move.start()
    bands = len(payloads)
    here = lax.axis_index("band")
    rows, hidden = latent.shape
    table = coef.shape[0]
    variables = proj.shape[0]
    proj_pad[...] = jnp.zeros_like(proj_pad)
    for move in moves[:3]:
        move.wait()
    proj_pad[0:variables, :] = proj[...]
    wide = latent[...].astype(F32)
    scale = coef[...].astype(F32)
    for q in range(table):
        products[q * rows : (q + 1) * rows, :] = (wide * scale[q : q + 1, :]).astype(BF16)
    projected = dot(proj_pad[...], products[...], 1, 1)
    for move in moves[3:]:
        move.wait()
    for i in range(bands):
        there = lax.bitwise_xor(here, i)
        ids = weight[here, pl.ds(there, 1), :] * rows + source[here, pl.ds(there, 1), :]
        pair_ids[i] = ids
        pack(payloads[i], pick(projected, ids), target[there, :, :].astype(F32), variables)


def predict_kernel(variables, *refs):
    *payloads, target, predicted = refs
    payloads = payloads[::-1]
    bands = len(payloads)
    here = lax.axis_index("band")
    total = 0.0
    for i in range(bands):
        there = lax.bitwise_xor(here, i)
        arrived, _ = unpack(payloads[i], variables, target.shape[2])
        total = total + dot(parts(arrived), hot(target[there, :, :], predicted.shape[1]), 1, 1)
    predicted[...] = whole(total)


def count_kernel(variables, cells_dev, pair_ids, *refs):
    *payloads, counts = refs
    payloads = payloads[::-1]
    for i, payload in enumerate(payloads):
        cells = unpack(payload, variables, pair_ids.shape[2])[1].astype(jnp.int32)
        block = dot(hot(pair_ids[i], counts.shape[0]), hot(cells, cells_dev), 1, 1)
        counts[:, i * cells_dev : (i + 1) * cells_dev] = block.astype(BF16)


def grade_kernel(pair_coef, target, area, var_weight, *refs):
    *predicted, grad, rows = refs
    members = len(predicted)
    here = lax.bitwise_xor(lax.axis_index("member"), 1)
    variables = target.shape[0]
    wanted = target[...]
    spots = lax.broadcasted_iota(jnp.int32, (variables, variables), 0)
    same = spots == lax.broadcasted_iota(jnp.int32, (variables, variables), 1)
    column = jnp.sum(jnp.where(same, var_weight[...], 0.0), axis=1, keepdims=True)
    weights = column * area[...]
    values = [ref[0:variables, :] for ref in predicted]
    own = values[0]
    slopes = 0.0
    for other in values[1:]:
        slopes = slopes + soft_slope(own - other)
    grad_pred = weights * (soft_slope(own - wanted) - pair_coef * slopes)
    for bit in range(members.bit_length() - 1):
        flip = lax.bitwise_and(lax.shift_right_logical(here, bit), 1) == 1
        ordered = list(values)
        for i in range(members):
            if not i >> bit & 1:
                first, second = values[i], values[i ^ (1 << bit)]
                ordered[i] = jnp.where(flip, second, first)
                ordered[i ^ (1 << bit)] = jnp.where(flip, first, second)
        values = ordered
    loss = 0.0
    spread = 0.0
    for m in range(members):
        loss = loss + soft_abs(values[m] - wanted)
        for k in range(m + 1, members):
            spread = spread + soft_abs(values[m] - values[k])
    total = jnp.sum(weights * (loss - pair_coef * spread), axis=(0, 1), keepdims=True)
    lane = lax.broadcasted_iota(jnp.int32, rows.shape, 1)
    pieces = [piece.astype(F32) for piece in pieces_of(total)]
    rows[...] = jnp.where(lane == 0, pieces[0], jnp.where(lane == 1, pieces[1], jnp.where(lane == 2, pieces[2], 0.0)))
    rows[0:variables, :] = grad_pred
    grad[...] = rows[...].astype(BF16)


def back_to_pairs(grad, proj, counts):
    return dot(grad, proj, 0, 0).astype(BF16), dot(grad, counts, 1, 1)


def only_grads(arrived, variables):
    row = lax.broadcasted_iota(jnp.int32, arrived.shape, 0)
    return jnp.where(row < variables, arrived.astype(F32), 0.0).astype(BF16)


def early_kernel(index, variables, proj, counts, grad, *refs):
    *before, pair_grad, block, cell_grad = refs
    cells_dev = grad.shape[1]
    own = counts[:, index * cells_dev : (index + 1) * cells_dev]
    cell_grad[...], pairs_here = back_to_pairs(only_grads(grad[...], variables), proj[...], own)
    pair_grad[...] = before[0][...] + pairs_here if before else pairs_here
    step = 256
    for h in range(0, block.shape[1], step):
        here = dot(own, cell_grad[:, h : h + step], 1, 0)
        block[:, h : h + step] = before[1][:, h : h + step] + here if before else here


def backward_kernel(members, variables, early, sent, scales, latent, coef, proj, counts, products, *refs):
    near_pair_grad, near_block, *rest = refs
    bands = lax.axis_size("band")
    grads, rest = rest[:bands], rest[bands:]
    latent_grad, sums, *all_pairs, cell_grad, wide_pairs = rest
    scale_proj, scale_coef = scales
    side = half_here(members, bands)
    rows, half = latent_grad.shape
    table = coef.shape[0]
    cells_dev = grads[0].shape[1]
    padded = grads[0].shape[0]
    base = (1 - side if sent else side) * half
    here = pl.ds(pl.multiple_of(base, half), half)
    wide_pairs[...] = near_pair_grad[...]
    for i in range(bands):
        if i not in early:
            grad = only_grads(grads[i][...], variables)
            spot = slice((i - 1) * cells_dev, i * cells_dev)
            cell_grad[spot, :] = dot(grad, proj[:, here], 0, 0).astype(BF16)
            if sent:
                wide_pairs[...] += dot(grad, counts[:, i * cells_dev : (i + 1) * cells_dev], 1, 1)
    if sent:
        all_pairs[0][...] = wide_pairs[...]
    sums[0:padded, :] = whole(dot(parts(wide_pairs[...]), products[:, here], 1, 0)) * scale_proj
    step = 256
    for h in range(0, half, step):
        spot = pl.ds(pl.multiple_of(base + h, step), step)
        block = near_block[:, spot] + dot(
            counts[:, cells_dev : cells_dev + cell_grad.shape[0]], cell_grad[:, h : h + step], 1, 0
        )
        wide = latent[:, spot].astype(F32)
        scale = coef[:, spot].astype(F32)
        into_latent = 0.0
        for q in range(table):
            piece = block[q * rows : (q + 1) * rows, :]
            into_latent = into_latent + piece * scale[q : q + 1, :]
            sums[padded + q : padded + q + 1, h : h + step] = (
                jnp.sum(piece * wide, axis=0, keepdims=True) * scale_coef
            )
        latent_grad[:, h : h + step] = into_latent.astype(BF16)


def loss_kernel(variables, scale, *refs):
    *grads, mean_loss = refs
    band = lax.axis_index("band")
    lane = lax.broadcasted_iota(jnp.int32, (1, 128), 1)
    losses = jnp.zeros((1, 128), F32)
    for i, grad in enumerate(grads):
        arrived = grad[...].astype(F32)
        loss = jnp.sum(arrived[variables : variables + 1, 0:128], axis=1, keepdims=True)
        losses = losses + jnp.where(lane == lax.bitwise_xor(band, i), loss, 0.0)
    mean_loss[...] = jnp.sum(losses, axis=1, keepdims=True) * scale


def write_half(side, summed, proj_out, coef_out, proj, leaves):
    half = summed.shape[1]
    spot = pl.ds(pl.multiple_of(side * half, half), half)
    proj[...] = summed[0 : proj.shape[0], :]
    moves = [
        pltpu.make_async_copy(summed.at[summed.shape[0] - coef_out.shape[0] :, :], coef_out.at[:, spot], leaves.at[0]),
        pltpu.make_async_copy(proj, proj_out.at[:, spot], leaves.at[1]),
    ]
    for move in moves:
        move.start()
    return moves


def write_kernel(members, bands, summed, latent_here, latent_there, mean_loss, *refs):
    latent_out, proj_out, coef_out, loss_out, proj, leaves = refs
    side = half_here(members, bands)
    moves = write_half(side, summed, proj_out, coef_out, proj, leaves)
    half = latent_here.shape[1]
    here = pl.ds(pl.multiple_of(side * half, half), half)
    there = pl.ds(pl.multiple_of((1 - side) * half, half), half)
    more = [
        (latent_here, latent_out.at[:, here]),
        (latent_there, latent_out.at[:, there]),
        (mean_loss, loss_out),
    ]
    for n, move in enumerate(more):
        moves.append(pltpu.make_async_copy(*move, leaves.at[n + 2]))
        moves[-1].start()
    for move in moves:
        move.wait()


def write_rest_kernel(members, bands, proj_in, coef_in, summed, proj_out, coef_out, proj, leaves):
    side = half_here(members, bands)
    for move in write_half(1 - side, summed, proj_out, coef_out, proj, leaves):
        move.wait()


def call(kernel, outs, operands, scratch=(), flops=0, source=VMEM, sink=VMEM):
    if source is HBM:
        operands = [pltpu.with_memory_space_constraint(x, pltpu.HBM) for x in operands]
    return pl.pallas_call(
        kernel,
        out_shape=outs,
        in_specs=[source] * len(operands),
        out_specs=[sink] * len(outs),
        scratch_shapes=list(scratch),
        compiler_params=PARAMS,
        cost_estimate=pl.CostEstimate(flops=flops, bytes_accessed=1 << 20, transcendentals=0),
    )(*operands)


def shape(*dims, dtype=F32):
    return jax.ShapeDtypeStruct(dims, dtype)


def local(
    latent,
    coef_table,
    out_proj,
    target,
    cell_area,
    var_weight,
    edge_source,
    edge_target,
    edge_weight,
):
    latent_rows = latent[0]
    rows, hidden = latent_rows.shape
    bands = lax.axis_size("band")
    members = lax.axis_size("member")
    variables, cells_dev = target.shape
    cells_all = cells_dev * bands
    table = coef_table.shape[0]
    slots = edge_source.shape[2]
    pairs = table * rows
    padded = up(variables + 1, 16)
    pair_coef = FAIR_ALPHA / (members - 1) + (1.0 - FAIR_ALPHA) / members

    *payloads, _, proj_pad, products, pair_ids, cell_ids, wanted, area, factor = call(
        project_kernel,
        [shape(*packed_shape(variables, slots))] * bands
        + [
            shape(variables, hidden, dtype=BF16),
            shape(padded, hidden, dtype=BF16),
            shape(pairs, hidden, dtype=BF16),
            shape(bands, 1, slots, dtype=jnp.int32),
            shape(bands, 1, slots, dtype=jnp.int32),
            shape(variables, cells_dev),
            shape(1, cells_dev),
            shape(1, variables),
        ],
        (
            latent_rows,
            coef_table,
            out_proj,
            edge_source,
            edge_weight,
            edge_target,
            target,
            cell_area.reshape(1, -1),
            var_weight.reshape(1, -1),
        ),
        [
            pltpu.VMEM((rows, hidden), BF16),
            pltpu.VMEM((table, hidden), BF16),
            pltpu.VMEM(edge_source.shape, jnp.int32),
            pltpu.VMEM(edge_weight.shape, jnp.int32),
            pltpu.SemaphoreType.DMA((9,)),
        ],
        source=HBM,
    )
    arrived = [cross(payloads[i], 1, i) for i in range(bands)][::-1]
    (predicted,) = call(
        functools.partial(predict_kernel, variables),
        [shape(up(variables, 8), cells_dev)],
        (*arrived, cell_ids),
    )
    (counts,) = call(
        functools.partial(count_kernel, variables, cells_dev),
        [shape(pairs, cells_all, dtype=BF16)],
        (pair_ids, *arrived),
        flops=2 * pairs * slots * cells_all,
    )
    members_here = [predicted, swap(predicted, "member", 1)]
    for i in range(2, members, 2):
        far = cross(predicted, i + 1, 0)
        if i == 2:
            far, counts = lax.optimization_barrier((far, counts))
        members_here += [swap(far, "member", 1), far]
    (grad,) = call(
        functools.partial(grade_kernel, pair_coef),
        [shape(padded, cells_dev, dtype=BF16)],
        (wanted, area, factor, *members_here),
        [pltpu.VMEM((padded, cells_dev), F32)],
    )
    grads = [cross(grad, 1, i) for i in range(bands)]
    early = sorted({0, bands - 1})
    sums = ()
    for index in early:
        sums = call(
            functools.partial(early_kernel, index, variables),
            [shape(padded, pairs), shape(pairs, hidden)],
            (proj_pad, counts, grads[index], *sums),
            [pltpu.VMEM((cells_dev, hidden), BF16)],
            flops=2 * pairs * cells_dev * hidden,
        )
    half = hidden // 2
    scales = (
        1.0 / math.sqrt(members * cells_all),
        1.0 / math.sqrt(members * cells_all * K),
    )
    pair_grad, block = sums

    def half_back(sent, pair_grad):
        return call(
            functools.partial(backward_kernel, members, variables, early, sent, scales),
            [shape(rows, half, dtype=BF16), shape(padded + table, half)] + [shape(padded, pairs)] * sent,
            (latent_rows, coef_table, proj_pad, counts, products, pair_grad, block, *grads),
            [
                pltpu.VMEM((cells_all - len(early) * cells_dev, half), BF16),
                pltpu.VMEM((padded, pairs), F32),
            ],
            flops=2 * pairs * cells_all * half,
        )

    latent_there, send, pair_grad = half_back(True, pair_grad)
    latent_here, keep = half_back(False, pair_grad)
    (mean_loss,) = call(
        functools.partial(loss_kernel, variables, 1.0 / (members * variables * cells_all)),
        [shape(1, 1)],
        grads,
    )
    total = keep + swap(send, "member", 1)
    step = 2
    while step < members:
        rounded = total.astype(BF16)
        far = cross(rounded, step + 1, 0)
        if step == 2:
            far, mean_loss = lax.optimization_barrier((far, mean_loss))
        total = rounded.astype(F32) + far.astype(F32)
        step *= 2
    step = 1
    while step < bands:
        rounded = total.astype(BF16)
        total = rounded.astype(F32) + cross(rounded, odd(step), step).astype(F32)
        if 2 * step < bands:
            far = [cross(rounded, odd(step * k), step * k).astype(F32) for k in (2, 3)]
            total = total + (far[0] + far[1])
        step *= 4
    other = swap(total, "member", 1)
    latent_out, proj_grad, coef_grad, loss_out = call(
        functools.partial(write_kernel, members, bands),
        [
            shape(rows, hidden, dtype=BF16),
            shape(variables, hidden),
            shape(table, hidden),
            shape(1, 1),
        ],
        (total, latent_here, latent_there, mean_loss),
        [pltpu.VMEM((variables, half), F32), pltpu.SemaphoreType.DMA((5,))],
        sink=HBM,
    )
    proj_grad, coef_grad = pl.pallas_call(
        functools.partial(write_rest_kernel, members, bands),
        out_shape=[shape(variables, hidden), shape(table, hidden)],
        in_specs=[HBM, HBM, VMEM],
        out_specs=[HBM, HBM],
        scratch_shapes=[pltpu.VMEM((variables, half), F32), pltpu.SemaphoreType.DMA((2,))],
        input_output_aliases={0: 0, 1: 1},
        compiler_params=PARAMS,
    )(proj_grad, coef_grad, other)
    return (latent_out[None], proj_grad, coef_grad, loss_out.reshape(1))


def solution(mesh):
    placed = (
        P(("groups", "member"), "band", None),
        P(),
        P(),
        P(None, ("groups", "band")),
        P("band"),
        P(),
        P(),
        P(None, "band", None),
        P(),
    )
    return jax.shard_map(
        local,
        mesh=mesh,
        in_specs=placed,
        out_specs=(
            P(("groups", "member"), "band", None),
            P("groups", None),
            P("groups", None),
            P("groups"),
        ),
        check_vma=False,
    )
```

```python
import functools
import math

import jax
import jax.numpy as jnp
from jax import lax
from jax.experimental import pallas as pl
from jax.experimental.pallas import tpu as pltpu
from jax.sharding import PartitionSpec as P

K = 4
LANES = 128
FAIR_ALPHA = 0.95
SOFTNESS = 0.1
F32 = jnp.float32
BF16 = jnp.bfloat16
VMEM = pl.BlockSpec(memory_space=pltpu.VMEM)
HBM = pl.BlockSpec(memory_space=pltpu.HBM)
PARAMS = pltpu.CompilerParams(vmem_limit_bytes=24 * 1024 * 1024)


def swap(shard, axis, mask):
    peers = lax.axis_size(axis)
    return lax.ppermute(shard, axis, [(i, i ^ mask) for i in range(peers)])


def cross(shard, member_mask, band_mask):
    members, bands = lax.axis_size("member"), lax.axis_size("band")
    pairs = [
        (m * bands + b, (m ^ member_mask) * bands + (b ^ band_mask))
        for m in range(members)
        for b in range(bands)
    ]
    return lax.ppermute(shard, ("member", "band"), pairs)


def odd(value):
    return value.bit_count() & 1


def parity(index, peers):
    found = 0
    for bit in range(peers.bit_length() - 1):
        found = lax.bitwise_xor(found, lax.bitwise_and(lax.shift_right_logical(index, bit), 1))
    return found


def half_here(members, bands):
    return lax.bitwise_xor(parity(lax.axis_index("member"), members), parity(lax.axis_index("band"), bands))


def soft_abs(values):
    return jnp.sqrt(values * values + SOFTNESS * SOFTNESS) - SOFTNESS


def soft_slope(values):
    return values * lax.rsqrt(values * values + SOFTNESS * SOFTNESS)


def up(size, unit):
    return -(-size // unit) * unit


def dot(left, right, left_dim, right_dim):
    return lax.dot_general(
        left, right, (((left_dim,), (right_dim,)), ((), ())), preferred_element_type=F32
    )


def pieces_of(values):
    high = values.astype(BF16)
    rest = values - high.astype(F32)
    mid = rest.astype(BF16)
    low = (rest - mid.astype(F32)).astype(BF16)
    return high, mid, low


def parts(values):
    return jnp.concatenate(pieces_of(values), axis=0)


def whole(stacked):
    rows = stacked.shape[0] // 3
    return (stacked[:rows] + stacked[rows : 2 * rows]) + stacked[2 * rows :]


def hot(ids, size):
    rows = lax.broadcasted_iota(jnp.int32, (size, ids.shape[1]), 0)
    return jnp.where(rows == ids, 1.0, 0.0).astype(BF16)


def pick(table, ids):
    rows, size = table.shape
    slots = ids.shape[1]
    if slots % LANES or size % LANES:
        return [whole(dot(parts(table), hot(ids, size), 1, 0))]
    pieces = []
    for first in range(0, slots, LANES):
        chosen = jnp.broadcast_to(ids[:, first : first + LANES], (rows, LANES))
        lane = lax.rem(chosen, LANES)
        block = lax.div(chosen, LANES)
        found = jnp.zeros((rows, LANES), F32)
        for start in range(0, size, LANES):
            there = jnp.take_along_axis(table[:, start : start + LANES], lane, axis=1, mode="promise_in_bounds")
            found = jnp.where(block == start // LANES, there, found)
        pieces.append(found)
    return pieces


def packed_shape(variables, slots):
    pieces = slots // LANES if slots % LANES == 0 else 1
    return up(pieces * (variables + 1), 8), slots // pieces


def pack(payload, pieces, cells, variables):
    lanes = payload.shape[1]
    full = variables // 8 * 8
    base = len(pieces) * full
    payload[base:, :] = jnp.zeros((payload.shape[0] - base, lanes), F32)
    for n, piece in enumerate(pieces):
        payload[n * full : (n + 1) * full, :] = piece[0:full]
        row = base + n * (variables + 1 - full)
        payload[row : row + variables - full, :] = piece[full:variables]
        payload[row + variables - full : row + variables - full + 1, :] = cells[:, n * lanes : (n + 1) * lanes]


def unpack(payload, variables, slots):
    lanes = payload.shape[1]
    full = variables // 8 * 8
    base = slots // lanes * full
    values, cells = [], []
    for n in range(slots // lanes):
        row = base + n * (variables + 1 - full)
        piece = payload[n * full : (n + 1) * full, :]
        for extra in range(variables - full):
            here = lax.broadcasted_iota(jnp.int32, (8, lanes), 0) == extra
            one = jnp.where(here, payload[row + extra : row + extra + 1, :], 0.0)
            tail = one if extra == 0 else tail + one
        values.append(jnp.concatenate([piece, tail], axis=0) if variables > full else piece)
        cells.append(payload[row + variables - full : row + variables - full + 1, :])
    if len(values) == 1:
        return values[0], cells[0]
    return jnp.concatenate(values, axis=1), jnp.concatenate(cells, axis=1)


def project_kernel(*refs):
    (latent_in, coef_in, proj_in, source_in, weight_in, target_in, wanted_in, area_in, factor_in, *rest) = refs
    *payloads, proj, proj_pad, products, pair_ids, target, wanted, area, factor = rest[:-5]
    latent, coef, source, weight, arrivals = rest[-5:]
    moves = [
        pltpu.make_async_copy(there, here, arrivals.at[n])
        for n, (there, here) in enumerate(
            [
                (latent_in, latent),
                (coef_in, coef),
                (proj_in, proj),
                (source_in, source),
                (weight_in, weight),
                (target_in, target),
                (wanted_in, wanted),
                (area_in, area),
                (factor_in, factor),
            ]
        )
    ]
    for move in moves:
        move.start()
    bands = len(payloads)
    here = lax.axis_index("band")
    rows, hidden = latent.shape
    table = coef.shape[0]
    variables = proj.shape[0]
    proj_pad[...] = jnp.zeros_like(proj_pad)
    for move in moves[:3]:
        move.wait()
    proj_pad[0:variables, :] = proj[...]
    wide = latent[...].astype(F32)
    scale = coef[...].astype(F32)
    for q in range(table):
        products[q * rows : (q + 1) * rows, :] = (wide * scale[q : q + 1, :]).astype(BF16)
    projected = dot(proj_pad[...], products[...], 1, 1)
    for move in moves[3:]:
        move.wait()
    for i in range(bands):
        there = lax.bitwise_xor(here, i)
        ids = weight[here, pl.ds(there, 1), :] * rows + source[here, pl.ds(there, 1), :]
        pair_ids[i] = ids
        pack(payloads[i], pick(projected, ids), target[there, :, :].astype(F32), variables)


def predict_kernel(variables, *refs):
    *payloads, target, predicted = refs
    payloads = payloads[::-1]
    bands = len(payloads)
    here = lax.axis_index("band")
    total = 0.0
    for i in range(bands):
        there = lax.bitwise_xor(here, i)
        arrived, _ = unpack(payloads[i], variables, target.shape[2])
        total = total + dot(parts(arrived), hot(target[there, :, :], predicted.shape[1]), 1, 1)
    predicted[...] = whole(total)


def count_kernel(variables, cells_dev, pair_ids, *refs):
    *payloads, counts = refs
    payloads = payloads[::-1]
    for i, payload in enumerate(payloads):
        cells = unpack(payload, variables, pair_ids.shape[2])[1].astype(jnp.int32)
        block = dot(hot(pair_ids[i], counts.shape[0]), hot(cells, cells_dev), 1, 1)
        counts[:, i * cells_dev : (i + 1) * cells_dev] = block.astype(BF16)


def grade_kernel(pair_coef, target, area, var_weight, *refs):
    *predicted, grad, rows = refs
    members = len(predicted)
    here = lax.bitwise_xor(lax.axis_index("member"), 1)
    variables = target.shape[0]
    wanted = target[...]
    spots = lax.broadcasted_iota(jnp.int32, (variables, variables), 0)
    same = spots == lax.broadcasted_iota(jnp.int32, (variables, variables), 1)
    column = jnp.sum(jnp.where(same, var_weight[...], 0.0), axis=1, keepdims=True)
    weights = column * area[...]
    values = [ref[0:variables, :] for ref in predicted]
    own = values[0]
    slopes = 0.0
    for other in values[1:]:
        slopes = slopes + soft_slope(own - other)
    grad_pred = weights * (soft_slope(own - wanted) - pair_coef * slopes)
    for bit in range(members.bit_length() - 1):
        flip = lax.bitwise_and(lax.shift_right_logical(here, bit), 1) == 1
        ordered = list(values)
        for i in range(members):
            if not i >> bit & 1:
                first, second = values[i], values[i ^ (1 << bit)]
                ordered[i] = jnp.where(flip, second, first)
                ordered[i ^ (1 << bit)] = jnp.where(flip, first, second)
        values = ordered
    loss = 0.0
    spread = 0.0
    for m in range(members):
        loss = loss + soft_abs(values[m] - wanted)
        for k in range(m + 1, members):
            spread = spread + soft_abs(values[m] - values[k])
    total = jnp.sum(weights * (loss - pair_coef * spread), axis=(0, 1), keepdims=True)
    lane = lax.broadcasted_iota(jnp.int32, rows.shape, 1)
    pieces = [piece.astype(F32) for piece in pieces_of(total)]
    rows[...] = jnp.where(lane == 0, pieces[0], jnp.where(lane == 1, pieces[1], jnp.where(lane == 2, pieces[2], 0.0)))
    rows[0:variables, :] = grad_pred
    grad[...] = rows[...].astype(BF16)


def back_to_pairs(grad, proj, counts):
    return dot(grad, proj, 0, 0).astype(BF16), dot(grad, counts, 1, 1)


def only_grads(arrived, variables):
    row = lax.broadcasted_iota(jnp.int32, arrived.shape, 0)
    return jnp.where(row < variables, arrived.astype(F32), 0.0).astype(BF16)


def early_kernel(index, variables, proj, counts, grad, *refs):
    *before, pair_grad, block, cell_grad = refs
    cells_dev = grad.shape[1]
    own = counts[:, index * cells_dev : (index + 1) * cells_dev]
    cell_grad[...], pairs_here = back_to_pairs(only_grads(grad[...], variables), proj[...], own)
    pair_grad[...] = before[0][...] + pairs_here if before else pairs_here
    step = 256
    for h in range(0, block.shape[1], step):
        here = dot(own, cell_grad[:, h : h + step], 1, 0)
        block[:, h : h + step] = before[1][:, h : h + step] + here if before else here


def backward_kernel(members, variables, early, sent, scales, latent, coef, proj, counts, products, *refs):
    near_pair_grad, near_block, *rest = refs
    bands = lax.axis_size("band")
    grads, rest = rest[:bands], rest[bands:]
    latent_grad, sums, *all_pairs, cell_grad, wide_pairs = rest
    scale_proj, scale_coef = scales
    side = half_here(members, bands)
    rows, half = latent_grad.shape
    table = coef.shape[0]
    cells_dev = grads[0].shape[1]
    padded = grads[0].shape[0]
    base = (1 - side if sent else side) * half
    here = pl.ds(pl.multiple_of(base, half), half)
    wide_pairs[...] = near_pair_grad[...]
    for i in range(bands):
        if i not in early:
            grad = only_grads(grads[i][...], variables)
            spot = slice((i - 1) * cells_dev, i * cells_dev)
            cell_grad[spot, :] = dot(grad, proj[:, here], 0, 0).astype(BF16)
            if sent:
                wide_pairs[...] += dot(grad, counts[:, i * cells_dev : (i + 1) * cells_dev], 1, 1)
    if sent:
        all_pairs[0][...] = wide_pairs[...]
    sums[0:padded, :] = whole(dot(parts(wide_pairs[...]), products[:, here], 1, 0)) * scale_proj
    step = 256
    for h in range(0, half, step):
        spot = pl.ds(pl.multiple_of(base + h, step), step)
        block = near_block[:, spot] + dot(
            counts[:, cells_dev : cells_dev + cell_grad.shape[0]], cell_grad[:, h : h + step], 1, 0
        )
        wide = latent[:, spot].astype(F32)
        scale = coef[:, spot].astype(F32)
        into_latent = 0.0
        for q in range(table):
            piece = block[q * rows : (q + 1) * rows, :]
            into_latent = into_latent + piece * scale[q : q + 1, :]
            sums[padded + q : padded + q + 1, h : h + step] = (
                jnp.sum(piece * wide, axis=0, keepdims=True) * scale_coef
            )
        latent_grad[:, h : h + step] = into_latent.astype(BF16)


def loss_kernel(members, variables, scale, latent_here, latent_there, *refs):
    *grads, mean_loss, latent_out, leaves = refs
    side = half_here(members, len(grads))
    half = latent_here.shape[1]
    here = pl.ds(pl.multiple_of(side * half, half), half)
    there = pl.ds(pl.multiple_of((1 - side) * half, half), half)
    moves = [
        pltpu.make_async_copy(latent_here, latent_out.at[:, here], leaves.at[0]),
        pltpu.make_async_copy(latent_there, latent_out.at[:, there], leaves.at[1]),
    ]
    for move in moves:
        move.start()
    band = lax.axis_index("band")
    lane = lax.broadcasted_iota(jnp.int32, (1, 128), 1)
    losses = jnp.zeros((1, 128), F32)
    for i, grad in enumerate(grads):
        arrived = grad[...].astype(F32)
        loss = jnp.sum(arrived[variables : variables + 1, 0:128], axis=1, keepdims=True)
        losses = losses + jnp.where(lane == lax.bitwise_xor(band, i), loss, 0.0)
    mean_loss[...] = jnp.sum(losses, axis=1, keepdims=True) * scale
    for move in moves:
        move.wait()


def write_half(side, summed, proj_out, coef_out, proj, leaves):
    half = summed.shape[1]
    spot = pl.ds(pl.multiple_of(side * half, half), half)
    proj[...] = summed[0 : proj.shape[0], :]
    moves = [
        pltpu.make_async_copy(summed.at[summed.shape[0] - coef_out.shape[0] :, :], coef_out.at[:, spot], leaves.at[0]),
        pltpu.make_async_copy(proj, proj_out.at[:, spot], leaves.at[1]),
    ]
    for move in moves:
        move.start()
    return moves


def write_kernel(members, bands, summed, mean_loss, *refs):
    proj_out, coef_out, loss_out, proj, leaves = refs
    side = half_here(members, bands)
    moves = write_half(side, summed, proj_out, coef_out, proj, leaves)
    moves.append(pltpu.make_async_copy(mean_loss, loss_out, leaves.at[2]))
    moves[-1].start()
    for move in moves:
        move.wait()


def write_rest_kernel(members, bands, proj_in, coef_in, summed, proj_out, coef_out, proj, leaves):
    side = half_here(members, bands)
    for move in write_half(1 - side, summed, proj_out, coef_out, proj, leaves):
        move.wait()


def call(kernel, outs, operands, scratch=(), flops=0, source=VMEM, sink=VMEM):
    if source is HBM:
        operands = [pltpu.with_memory_space_constraint(x, pltpu.HBM) for x in operands]
    return pl.pallas_call(
        kernel,
        out_shape=outs,
        in_specs=[source] * len(operands),
        out_specs=[sink] * len(outs),
        scratch_shapes=list(scratch),
        compiler_params=PARAMS,
        cost_estimate=pl.CostEstimate(flops=flops, bytes_accessed=1 << 20, transcendentals=0),
    )(*operands)


def shape(*dims, dtype=F32):
    return jax.ShapeDtypeStruct(dims, dtype)


def local(
    latent,
    coef_table,
    out_proj,
    target,
    cell_area,
    var_weight,
    edge_source,
    edge_target,
    edge_weight,
):
    latent_rows = latent[0]
    rows, hidden = latent_rows.shape
    bands = lax.axis_size("band")
    members = lax.axis_size("member")
    variables, cells_dev = target.shape
    cells_all = cells_dev * bands
    table = coef_table.shape[0]
    slots = edge_source.shape[2]
    pairs = table * rows
    padded = up(variables + 1, 16)
    pair_coef = FAIR_ALPHA / (members - 1) + (1.0 - FAIR_ALPHA) / members

    *payloads, _, proj_pad, products, pair_ids, cell_ids, wanted, area, factor = call(
        project_kernel,
        [shape(*packed_shape(variables, slots))] * bands
        + [
            shape(variables, hidden, dtype=BF16),
            shape(padded, hidden, dtype=BF16),
            shape(pairs, hidden, dtype=BF16),
            shape(bands, 1, slots, dtype=jnp.int32),
            shape(bands, 1, slots, dtype=jnp.int32),
            shape(variables, cells_dev),
            shape(1, cells_dev),
            shape(1, variables),
        ],
        (
            latent_rows,
            coef_table,
            out_proj,
            edge_source,
            edge_weight,
            edge_target,
            target,
            cell_area.reshape(1, -1),
            var_weight.reshape(1, -1),
        ),
        [
            pltpu.VMEM((rows, hidden), BF16),
            pltpu.VMEM((table, hidden), BF16),
            pltpu.VMEM(edge_source.shape, jnp.int32),
            pltpu.VMEM(edge_weight.shape, jnp.int32),
            pltpu.SemaphoreType.DMA((9,)),
        ],
        source=HBM,
    )
    arrived = [cross(payloads[i], 1, i) for i in range(bands)][::-1]
    (predicted,) = call(
        functools.partial(predict_kernel, variables),
        [shape(up(variables, 8), cells_dev)],
        (*arrived, cell_ids),
    )
    (counts,) = call(
        functools.partial(count_kernel, variables, cells_dev),
        [shape(pairs, cells_all, dtype=BF16)],
        (pair_ids, *arrived),
        flops=2 * pairs * slots * cells_all,
    )
    members_here = [predicted, swap(predicted, "member", 1)]
    for i in range(2, members, 2):
        far = cross(predicted, i + 1, 0)
        if i == 2:
            far, counts = lax.optimization_barrier((far, counts))
        members_here += [swap(far, "member", 1), far]
    (grad,) = call(
        functools.partial(grade_kernel, pair_coef),
        [shape(padded, cells_dev, dtype=BF16)],
        (wanted, area, factor, *members_here),
        [pltpu.VMEM((padded, cells_dev), F32)],
    )
    grads = [cross(grad, 1, i) for i in range(bands)]
    early = sorted({0, bands - 1})
    sums = ()
    for index in early:
        sums = call(
            functools.partial(early_kernel, index, variables),
            [shape(padded, pairs), shape(pairs, hidden)],
            (proj_pad, counts, grads[index], *sums),
            [pltpu.VMEM((cells_dev, hidden), BF16)],
            flops=2 * pairs * cells_dev * hidden,
        )
    half = hidden // 2
    scales = (
        1.0 / math.sqrt(members * cells_all),
        1.0 / math.sqrt(members * cells_all * K),
    )
    pair_grad, block = sums

    def half_back(sent, pair_grad):
        return call(
            functools.partial(backward_kernel, members, variables, early, sent, scales),
            [shape(rows, half, dtype=BF16), shape(padded + table, half)] + [shape(padded, pairs)] * sent,
            (latent_rows, coef_table, proj_pad, counts, products, pair_grad, block, *grads),
            [
                pltpu.VMEM((cells_all - len(early) * cells_dev, half), BF16),
                pltpu.VMEM((padded, pairs), F32),
            ],
            flops=2 * pairs * cells_all * half,
        )

    latent_there, send, pair_grad = half_back(True, pair_grad)
    latent_here, keep = half_back(False, pair_grad)
    mean_loss, latent_out = pl.pallas_call(
        functools.partial(loss_kernel, members, variables, 1.0 / (members * variables * cells_all)),
        out_shape=[shape(1, 1), shape(rows, hidden, dtype=BF16)],
        in_specs=[VMEM] * (2 + bands),
        out_specs=[VMEM, HBM],
        scratch_shapes=[pltpu.SemaphoreType.DMA((2,))],
        compiler_params=PARAMS,
    )(latent_here, latent_there, *grads)
    total = keep + swap(send, "member", 1)
    step = 2
    while step < members:
        rounded = total.astype(BF16)
        far = cross(rounded, step + 1, 0)
        if step == 2:
            far, mean_loss = lax.optimization_barrier((far, mean_loss))
        total = rounded.astype(F32) + far.astype(F32)
        step *= 2
    step = 1
    while step < bands:
        rounded = total.astype(BF16)
        total = rounded.astype(F32) + cross(rounded, odd(step), step).astype(F32)
        if 2 * step < bands:
            far = [cross(rounded, odd(step * k), step * k).astype(F32) for k in (2, 3)]
            total = total + (far[0] + far[1])
        step *= 4
    other = swap(total, "member", 1)
    proj_grad, coef_grad, loss_out = call(
        functools.partial(write_kernel, members, bands),
        [
            shape(variables, hidden),
            shape(table, hidden),
            shape(1, 1),
        ],
        (total, mean_loss),
        [pltpu.VMEM((variables, half), F32), pltpu.SemaphoreType.DMA((3,))],
        sink=HBM,
    )
    proj_grad, coef_grad = pl.pallas_call(
        functools.partial(write_rest_kernel, members, bands),
        out_shape=[shape(variables, hidden), shape(table, hidden)],
        in_specs=[HBM, HBM, VMEM],
        out_specs=[HBM, HBM],
        scratch_shapes=[pltpu.VMEM((variables, half), F32), pltpu.SemaphoreType.DMA((2,))],
        input_output_aliases={0: 0, 1: 1},
        compiler_params=PARAMS,
    )(proj_grad, coef_grad, other)
    return (latent_out[None], proj_grad, coef_grad, loss_out.reshape(1))


def solution(mesh):
    placed = (
        P(("groups", "member"), "band", None),
        P(),
        P(),
        P(None, ("groups", "band")),
        P("band"),
        P(),
        P(),
        P(None, "band", None),
        P(),
    )
    return jax.shard_map(
        local,
        mesh=mesh,
        in_specs=placed,
        out_specs=(
            P(("groups", "member"), "band", None),
            P("groups", None),
            P("groups", None),
            P("groups"),
        ),
        check_vma=False,
    )
```
